512 devices in a mesh: tile: 8 (over x, core), mask: 2 (over z_hi), pencil: 32 (over y, z_lo).
Axes of the slice: x: 4, y: 4, z: 16 (z_hi: 2, z_lo: 8; z = z_hi * 8 + z_lo), core: 2. Of those that a mesh axis runs over, the one named last changes fastest.
Arguments:
- mask_field: float32 [8, 2, 4096, 4096], P('tile', 'mask', 'pencil'), may hold values from 0 to 1
- design_target: bfloat16 [8, 4096, 4096], P('tile', 'pencil'), may hold values from 0 to 1
- kernel_spectra: float32 [2, 4, 256, 256], P(None, None, 'pencil'), may hold values from -32 to 32
- support_radii: int32 [4], replicated, may hold values from 64 to 128
- edge_points: int32 [8, 3, 8192], P('tile', None, 'pencil'), may hold values from 0 to 4095, as said below
- point_weights: float32 [8, 8192], P('tile', 'pencil'), may hold values from 1 to 27
Outputs:
- updated_mask: bfloat16 [8, 2, 4096, 4096], P('tile', 'mask', 'pencil')
- total_loss: float32 [], replicated
The draws below stay inside these ranges and needn't reach their ends.
Inputs may be any that keep to these rules, and one draw needn't show every extreme that they name: edge_points[t, 0, i] is a row and edge_points[t, 1, i] a column of tile t; for i in the j-th aligned block of 256 points the row lies in j * 128 + 1 to j * 128 + 126, and every block reaches both ends; columns lie in 1 to 4094; edge_points[t, 2, i] is the normal code 0 to 3.
All inputs are finite; a program needn't handle non-finite values.
Results may differ from the reference program's by a relative error of at most 0.013.
Values may be sent and summed in bfloat16 or wider, within the bound.
A program may use at most 128 MiB of HBM per device.

```python
import math
import jax
import jax.numpy as jnp
from jax import lax

N = 4096
SPLIT = 64
INNER = 64
BANDS = 4
KEEP = 256
KERN = 4
PTS_DEV = 256
TILES = 8
MASKS = 2
ROWS = 128
PTS = 8192


def layout_cells(key):
    key = jax.random.fold_in(key, 7)
    cell_size = max(N // KEEP, 2)
    cell_total = N // cell_size
    levels = jax.random.randint(key, (TILES, MASKS, cell_total, cell_total), 0, 100)
    cell_rows = jnp.arange(cell_total, dtype=jnp.int32)
    chance = 20 + 40 * cell_rows // cell_total
    filled = (levels < chance[None, None, :, None]).astype(jnp.float32)
    return jnp.repeat(jnp.repeat(filled, cell_size, axis=2), cell_size, axis=3)


def point_rows(key):
    key = jax.random.fold_in(key, 9)
    local_rows = jax.random.randint(key, (TILES, PTS), 1, ROWS - 1)
    point_index = jnp.arange(PTS, dtype=jnp.int32)
    block_slot = point_index % PTS_DEV
    local_rows = jnp.where(block_slot[None] == 0, 1, jnp.where(block_slot[None] == 1, ROWS - 2, local_rows))
    return (point_index // PTS_DEV)[None] * ROWS + local_rows


def draw_mask_field(key, part):
    design = layout_cells(key)
    key = jax.random.fold_in(key, 1)
    key_rough, key_order = jax.random.split(key, 2)
    order = jax.random.permutation(key_order, TILES * MASKS).reshape(TILES, MASKS)
    level = order.astype(jnp.float32) / max(TILES * MASKS - 1, 1)
    amplitude = (0.125 ** level)[:, :, None, None]
    roughness = jax.random.uniform(key_rough, design.shape, jnp.float32, -0.15, 0.15)
    return amplitude * (0.15 + 0.7 * design + roughness)


def draw_design_target(key, part):
    design = layout_cells(key)
    return jnp.max(design, axis=1).astype(jnp.bfloat16)


def draw_kernel_spectra(key, part):
    key = jax.random.fold_in(key, 3)
    key_shiftx, key_shifty, key_coef, key_rough = jax.random.split(key, 4)
    tap_count = 8
    reach = 4 * N // KEEP
    shift_x = jax.random.randint(key_shiftx, (KERN, tap_count), -reach, reach + 1)
    shift_y = jax.random.randint(key_shifty, (KERN, tap_count), -reach, reach + 1)
    coefs = jnp.clip(0.3 * jax.random.normal(key_coef, (2, KERN, tap_count), jnp.float32), -1.0, 1.0)
    roughness = jnp.clip(1.0 + 0.3 * jax.random.normal(key_rough, (2, KERN, KEEP, KEEP), jnp.float32), 0.1, 1.9)
    falloff = 0.4
    freqs = jnp.arange(KEEP, dtype=jnp.int32) - KEEP // 2
    phase_index = jnp.mod(freqs[None, None, None, :] * shift_x[:, :, None, None] + freqs[None, None, :, None] * shift_y[:, :, None, None], N)
    angle = 2.0 * math.pi / N * phase_index.astype(jnp.float32)
    coef_real = coefs[0][:, :, None, None]
    coef_imag = coefs[1][:, :, None, None]
    kernel_real = jnp.sum(coef_real * jnp.cos(angle) + coef_imag * jnp.sin(angle), axis=1)
    kernel_imag = jnp.sum(coef_imag * jnp.cos(angle) - coef_real * jnp.sin(angle), axis=1)
    freq_float = freqs.astype(jnp.float32)
    width = 1.0 * KEEP
    envelope = jnp.exp(-(freq_float[:, None] ** 2 + freq_float[None, :] ** 2) / (2.0 * width * width))
    kernel_scale = 1.0 / (1.0 + falloff * jnp.arange(KERN, dtype=jnp.float32))
    stacked = jnp.stack([kernel_real, kernel_imag]) * envelope[None, None] * kernel_scale[None, :, None, None]
    return stacked * roughness


def draw_edge_points(key, part):
    row_values = point_rows(key)
    key = jax.random.fold_in(key, 4)
    key_cols, key_normal = jax.random.split(key, 2)
    col_values = jax.random.randint(key_cols, (TILES, PTS), 1, N - 1)
    normal_codes = jax.random.randint(key_normal, (TILES, PTS), 0, 4)
    return jnp.stack([row_values, col_values, normal_codes], axis=1).astype(jnp.int32)


def draw_point_weights(key, part):
    row_values = point_rows(key)
    key = jax.random.fold_in(key, 5)
    base_weight = jnp.exp(jax.random.uniform(key, (TILES, PTS), jnp.float32, 0.0, math.log(3.0)))
    tile_range = jnp.arange(TILES, dtype=jnp.float32)[:, None] / max(TILES - 1, 1)
    rising = 3.0 ** (row_values.astype(jnp.float32) / N) * 3.0 ** tile_range
    return base_weight * rising


def set_ends(values, own_key, least, high):
    dims = values.shape
    place = [jax.random.randint(jax.random.fold_in(own_key, axis), (), 0, dims[axis]) for axis in range(len(dims))]
    values = values.at[tuple(place)].set(least)
    longest = dims.index(max(dims))
    place[longest] = (place[longest] + 1) % dims[longest]
    return values.at[tuple(place)].set(high)


def setup_inputs(seed: int = 0) -> dict:
    arg_keys = jax.random.split(jax.random.key(seed), 7)
    return {
        "mask_field": draw_mask_field(jax.random.fold_in(arg_keys[6], 71), 0),
        "design_target": draw_design_target(jax.random.fold_in(arg_keys[6], 71), 0),
        "kernel_spectra": draw_kernel_spectra(jax.random.fold_in(arg_keys[6], 71), 0),
        "support_radii": set_ends(jax.random.randint(arg_keys[3], (KERN,), KEEP // 4, KEEP // 2 + 1), jax.random.fold_in(arg_keys[3], 1), KEEP // 4, (KEEP // 2 + 1) - 1).astype(jnp.int32),
        "edge_points": draw_edge_points(jax.random.fold_in(arg_keys[6], 71), 0),
        "point_weights": draw_point_weights(jax.random.fold_in(arg_keys[6], 71), 0),
    }


STEEPNESS = 6.0
THRESHOLD = 0.5
STEP_SIZE = 0.2
EPSILON = 1e-06

def phase_pair(phase_index, period, direction):
    angle = 2.0 * math.pi / period * phase_index.astype(jnp.float32)
    return (jnp.cos(angle), direction * jnp.sin(angle))

def complex_table(phase_index, period, direction):
    cosine_table, sine_table = phase_pair(phase_index, period, direction)
    upper = jnp.stack([cosine_table, sine_table], axis=1)
    lower = jnp.stack([-sine_table, cosine_table], axis=1)
    return jnp.stack([upper, lower], axis=0).astype(jnp.bfloat16)

def joint_table(phase_index, direction):
    cosine_table, sine_table = phase_pair(phase_index, N, direction)
    upper = jnp.stack([cosine_table, sine_table])
    lower = jnp.stack([-sine_table, cosine_table])
    return jnp.stack([upper, lower]).astype(jnp.bfloat16)

def build_tables():
    inner_range = jnp.arange(INNER, dtype=jnp.int32)
    outer_range = jnp.arange(SPLIT, dtype=jnp.int32)
    band_range = jnp.arange(BANDS, dtype=jnp.int32) - BANDS // 2
    square_index = jnp.mod(inner_range[:, None] * inner_range[None, :], INNER)
    cross_index = jnp.mod(outer_range[:, None] * band_range[None, :], SPLIT)
    first_index = jnp.mod(inner_range[None, :, None] * inner_range[None, None, :] * SPLIT + outer_range[:, None, None] * inner_range[None, None, :], N)
    back_index = jnp.mod(band_range[None, :, None] * outer_range[None, None, :] * INNER + inner_range[:, None, None] * outer_range[None, None, :], N)
    ahead_first = joint_table(first_index, -1.0)
    ahead_last = complex_table(cross_index, SPLIT, -1.0)
    back_first = joint_table(back_index, 1.0)
    back_last = complex_table(square_index, INNER, 1.0)
    return (ahead_first, ahead_last, back_first, back_last)

def contract(form, left, right):
    return jnp.einsum(form, left.astype(jnp.float32), right.astype(jnp.float32), precision=lax.Precision.HIGHEST)

def forward_pass(values, tables, transposed):
    ahead_first, ahead_last, back_first, back_last = tables
    pieces, groups, batch_rows = (values.shape[0], values.shape[1], values.shape[2])
    split_form = values.reshape(pieces, groups, batch_rows, INNER, SPLIT)
    turned = contract('pgmba,pqabk->qgmak', split_form, ahead_first[:pieces]).astype(jnp.bfloat16)
    if transposed:
        return contract('pgmak,paqj->qgjkm', turned, ahead_last).reshape(2, groups, KEEP, batch_rows)
    return contract('pgmak,paqj->qgmjk', turned, ahead_last).reshape(2, groups, batch_rows, KEEP)

def inverse_pass(band_data, tables, transposed, pieces):
    ahead_first, ahead_last, back_first, back_last = tables
    groups = band_data.shape[1]
    if transposed:
        batch_rows = band_data.shape[3]
        split_form = band_data.reshape(2, groups, BANDS, INNER, batch_rows)
        turned = contract('pgjkm,pqkja->qgmak', split_form, back_first)
    else:
        batch_rows = band_data.shape[2]
        split_form = band_data.reshape(2, groups, batch_rows, BANDS, INNER)
        turned = contract('pgmjk,pqkja->qgmak', split_form, back_first)
    turned = turned.astype(jnp.bfloat16)
    result = contract('pgmak,pkqb->qgmba', turned, back_last[:, :, :pieces])
    return result.reshape(pieces, groups, batch_rows, N)

def product_band(spectra, spectrum, factor):
    kernel_real, kernel_imag = (spectra[0], spectra[1])
    mask_real, mask_imag = (spectrum[0], spectrum[1])
    return jnp.stack([(kernel_real * mask_real - kernel_imag * mask_imag) * factor, (kernel_real * mask_imag + kernel_imag * mask_real) * factor]).astype(jnp.bfloat16)

def adjoint_band(spectra, backs, factor):
    kernel_real, kernel_imag = (spectra[0], spectra[1])
    back_real, back_imag = (backs[0], backs[1])
    summed_real = lax.optimization_barrier(jnp.sum(kernel_real * back_real + kernel_imag * back_imag, axis=0)) * factor
    summed_imag = lax.optimization_barrier(jnp.sum(kernel_real * back_imag - kernel_imag * back_real, axis=0)) * factor
    return jnp.stack([summed_real, summed_imag])[:, None].astype(jnp.bfloat16)

def reference(mask_field, design_target, kernel_spectra, support_radii, edge_points, point_weights):
    tables = build_tables()
    freqs = jnp.arange(KEEP, dtype=jnp.int32) - KEEP // 2
    radius_sq = freqs[:, None] ** 2 + freqs[None, :] ** 2
    inside = (radius_sq[None] <= (support_radii ** 2)[:, None, None]).astype(jnp.float32)
    spectra = kernel_spectra * inside[None]
    goals = jnp.array([0.5, 1.0, 0.0], dtype=jnp.float32)[:, None]

    def kernel_fields(plane):
        image = plane.astype(jnp.bfloat16).reshape(1, 1, N, N)
        lined = forward_pass(image, tables, True).astype(jnp.bfloat16)
        spectrum = forward_pass(lined, tables, False)
        band_data = product_band(spectra, spectrum, 1.0 / (N * N))
        partial_value = inverse_pass(band_data, tables, False, 2).astype(jnp.bfloat16)

        def one_kernel(piece):
            return inverse_pass(piece[:, None], tables, True, 2).astype(jnp.bfloat16)[:, 0]
        stacked = lax.map(one_kernel, jnp.moveaxis(partial_value, 1, 0))
        return jnp.moveaxis(stacked, 0, 1)

    def resist_of(fields):
        wide_fields = fields.astype(jnp.float32)
        intensity = lax.optimization_barrier(jnp.sum(wide_fields * wide_fields, axis=(0, 1)))
        return jax.nn.sigmoid(STEEPNESS * (intensity - THRESHOLD)).astype(jnp.bfloat16)

    def adjoint(drive, fields):

        def one_kernel(piece):
            mixed = (drive.astype(jnp.float32)[None] * piece.astype(jnp.float32)).astype(jnp.bfloat16)[:, None]
            lined = forward_pass(mixed, tables, True).astype(jnp.bfloat16)
            return forward_pass(lined, tables, False)[:, 0]
        backs = jnp.moveaxis(lax.map(one_kernel, jnp.moveaxis(fields, 1, 0)), 0, 1)
        band_grad = adjoint_band(spectra, backs, 2.0 / (N * N))
        partial_value = inverse_pass(band_grad, tables, False, 2).astype(jnp.bfloat16)
        return inverse_pass(partial_value, tables, True, 1)[0, 0]

    def tile_step(carry, inputs):
        planes, target, points, weights = inputs
        fields_first = kernel_fields(planes[0])
        fields_second = kernel_fields(planes[1])
        resist_first = resist_of(fields_first).astype(jnp.float32)
        resist_second = resist_of(fields_second).astype(jnp.float32)
        union = resist_first + resist_second - resist_first * resist_second
        gap = union - target.astype(jnp.float32)
        edge_rows, edge_cols, normal = (points[0], points[1], points[2])
        step_row = (normal == 0).astype(jnp.int32) - (normal == 1).astype(jnp.int32)
        step_col = (normal == 2).astype(jnp.int32) - (normal == 3).astype(jnp.int32)
        places = jnp.stack([edge_rows * N + edge_cols, (edge_rows - step_row) * N + (edge_cols - step_col), (edge_rows + step_row) * N + (edge_cols + step_col)]).astype(jnp.int32)
        at_points = union.reshape(-1)[places]
        missed = at_points - goals
        tile_loss = jnp.sum(gap * gap) + jnp.sum(weights[None] * missed * missed)
        pushes = 2.0 * weights[None] * missed
        scattered = jnp.zeros((N * N,), jnp.float32).at[places.reshape(-1)].add(pushes.reshape(-1))
        grad_union = 2.0 * gap + scattered.reshape(N, N)
        drive_first = (grad_union * (1.0 - resist_second) * STEEPNESS * resist_first * (1.0 - resist_first)).astype(jnp.bfloat16)
        drive_second = (grad_union * (1.0 - resist_first) * STEEPNESS * resist_second * (1.0 - resist_second)).astype(jnp.bfloat16)
        gradients = jnp.stack([adjoint(drive_first, fields_first), adjoint(drive_second, fields_second)])
        return (carry + tile_loss, gradients)
    loss_sum, gradients = lax.scan(tile_step, jnp.zeros((), jnp.float32), (mask_field, design_target, edge_points, point_weights))
    squares = jnp.sum(gradients * gradients)
    spread = jnp.sqrt(squares / (TILES * MASKS * N * N) + EPSILON)
    updated_mask = (mask_field - STEP_SIZE * gradients / spread).astype(jnp.bfloat16)
    return (updated_mask, loss_sum / (TILES * N * N))
```

```python
import functools
import math

import jax
import jax.numpy as jnp
import numpy as np
from jax import lax
from jax.experimental import pallas as pl
from jax.experimental.pallas import tpu as pltpu
from jax.sharding import PartitionSpec as P
from ml_dtypes import bfloat16

N = 4096
KEEP = 256
HALF = 128
KERN = 4
ROWS = 128
SAMPLES = 512
PENCIL = 32
CHUNK = 512
PTS = 256
FIRST = 2
EPSILON = 1e-06
STEP_SIZE = 0.2
F32 = jnp.float32
BF16 = jnp.bfloat16
MESH = pl.DeviceIdType.MESH
VMEM = pltpu.VMEM
DMA = pltpu.SemaphoreType.DMA


def angles(first, second, period):
    return 2.0 * np.pi / period * ((first[:, None] * second[None, :]) % period)


@functools.cache
def tables():
    pixels = np.arange(N)
    freqs = np.arange(KEEP) - HALF
    half = np.arange(136)
    theta = angles(half, pixels, N)
    theta_cos, theta_sin = (np.cos(theta), np.sin(theta))
    theta_cos[129:], theta_sin[129:] = (0.0, 0.0)
    ahead = np.stack([theta_cos.reshape(17, 8, N), -theta_sin.reshape(17, 8, N)], axis=1).reshape(272, N)
    theta = angles(pixels, freqs, N)
    ahead_x = np.concatenate([np.cos(theta), np.sin(theta)], axis=1)
    theta_cos, theta_sin = (np.cos(theta), np.sin(theta))
    back_x = np.concatenate(
        [
            np.concatenate([theta_cos, -theta_sin], axis=1).reshape(PENCIL, ROWS, 512),
            np.concatenate([theta_sin, theta_cos], axis=1).reshape(PENCIL, ROWS, 512),
        ],
        axis=1,
    )
    theta = angles(np.abs(freqs), np.arange(SAMPLES), SAMPLES)
    sign = np.where(freqs < 0, -1.0, 1.0)[:, None]
    back_y = np.concatenate(
        [
            np.concatenate([np.cos(theta), sign * np.sin(theta)], axis=1),
            np.concatenate([-np.sin(theta), sign * np.cos(theta)], axis=1),
        ],
        axis=0,
    )
    shift = np.arange(N)
    bell = np.ones(N)
    for freq in range(1, 256):
        bell += 2.0 * np.cos(2.0 * np.pi / N * ((freq * shift) % N))
    bell /= SAMPLES
    bell += np.cos(2.0 * np.pi / N * ((256 * shift) % N)) / SAMPLES
    spread = bell[(pixels[None, :] - 8 * np.arange(SAMPLES)[:, None]) % N]
    pick = np.zeros((512, 256))
    for row in range(KEEP):
        a = abs(row - HALF)
        if a < HALF:
            pick[row, 16 * (a // 8) + a % 8] = 1.0
            pick[KEEP + row, 16 * (a // 8) + 8 + a % 8] = 1.0
    flip = np.zeros((KEEP, KEEP))
    for lane in range(1, KEEP):
        flip[KEEP - lane, lane] = 1.0
    return {
        "ahead": ahead.astype(bfloat16),
        "ahead_x": ahead_x.astype(bfloat16),
        "back_x": back_x.astype(bfloat16),
        "back_y": back_y.astype(bfloat16),
        "spread": spread.astype(bfloat16),
        "spread_t": np.ascontiguousarray(spread.T).astype(bfloat16),
        "pick": pick.astype(bfloat16),
        "merge": np.ascontiguousarray(pick.T).astype(bfloat16),
        "flip": flip.astype(bfloat16),
    }


def dot_nn(left, right):
    return lax.dot_general(left, right, (((1,), (0,)), ((), ())), preferred_element_type=F32)


def dot_nt(left, right):
    return lax.dot_general(left, right, (((1,), (1,)), ((), ())), preferred_element_type=F32)


def iota(shape, axis):
    return lax.broadcasted_iota(jnp.int32, shape, axis)


def each(low, high, body):
    def step(i, carry):
        body(i)
        return carry

    lax.fori_loop(low, high, step, 0)


def place():
    tile = lax.axis_index("tile")
    mask = lax.axis_index("mask")
    pencil = lax.axis_index("pencil")
    return tile, mask, pencil, pencil // 8, pencil % 8


def remote(src, dst, send, recv, where):
    return pltpu.make_async_remote_copy(
        src_ref=src, dst_ref=dst, send_sem=send, recv_sem=recv, device_id=where, device_id_type=MESH
    )


def step_kernel(
    mask_hbm, ahead_hbm, ahead_x_hbm, back_x_hbm, back_y_hbm, spread_hbm, target_hbm, spread_t_hbm,
    pick_ref, merge_ref, flip_ref, spectra_ref, points_ref, weights_ref, radii_ref,
    gradient_hbm, scale_out, loss_out,
    mask_ref, ahead_ref, ahead_x_ref, back_x, back_y, spread, target, spread_t,
    line_ref, lines_ref, seen, kern, slices, bands, fields, gap_ref, slope_ref, hot_ref, hot_t_ref,
    part_ref, gathered, summed, pieces, whole, note, notes, totals,
    load_sem, self_sem, kz_send, kz_recv, kx_send, kx_recv, kc_send, kc_recv,
    a_send, a_recv, sz_send, sz_recv, sy_send, sy_recv,
    cy_send, cy_recv, cz_send, cz_recv, dz_send, dz_recv, dy_send, dy_recv, e_send, e_recv, f_send, f_recv,
):
    tile, mask, pencil, y, z = place()
    chip, core = (tile // 2, tile % 2)
    owner = (z >= FIRST) & (z < FIRST + 4)
    column = z - FIRST
    load_mask = pltpu.make_async_copy(mask_hbm, mask_ref, load_sem.at[0])
    load_ahead = pltpu.make_async_copy(ahead_hbm, ahead_ref, load_sem.at[1])
    load_mask.start()
    load_ahead.start()
    barrier = pltpu.get_barrier_semaphore()

    def greet(where):
        pl.semaphore_signal(barrier, inc=1, device_id=where, device_id_type=MESH)

    def spot_of(d):
        spot = (mask * 8 + tile + d) % 16
        return spot, {"mask": spot // 8, "tile": spot % 8}

    each(1, 32, lambda d: greet({"pencil": (pencil + d) % 32}))
    each(1, 16, lambda d: greet(spot_of(d)[1]))
    each(1, 8, lambda d: greet({"mask": 1 - mask, "pencil": y * 8 + (z + d) % 8}))

    sub = iota((8, KEEP), 0)
    lane = iota((8, KEEP), 1)
    freq_u = lane - HALF
    freq_v = sub + pencil * 8 - HALF
    radius = freq_u * freq_u + freq_v * freq_v
    parts = []
    for c in range(2):
        for k in range(KERN):
            limit = radii_ref[k] * radii_ref[k]
            parts.append(jnp.where(radius <= limit, spectra_ref[c, k], 0.0))
    plain = jnp.concatenate(parts, axis=0)
    turned = dot_nn(plain.astype(BF16), flip_ref[...])
    sign = jnp.where(iota((64, KEEP), 0) < 32, 1.0, -1.0)
    low = jnp.where(pencil < 16, 1.0, 0.0).astype(F32)
    plain = low * (turned * sign) + (1.0 - low) * plain
    spare = (sub == 1) & (lane == 0) & (pencil == 16)
    for part in range(8):
        rows = plain[part * 8 : part * 8 + 8]
        rest = rows - rows.astype(BF16).astype(F32)
        rows = jnp.where(spare, rest[0:1, HALF : HALF + 1], rows)
        slices[part] = jnp.concatenate([rows[:, :HALF], rows[:, HALF:]], axis=0).astype(BF16)
    kern[tile, y, z] = slices[tile]

    point_rows = points_ref[0].astype(F32) - (pencil * ROWS).astype(F32)
    point_cols = points_ref[1].astype(F32)
    normal = points_ref[2]
    step_row = jnp.where(normal == 0, 1.0, 0.0) - jnp.where(normal == 1, 1.0, 0.0)
    step_col = jnp.where(normal == 2, 1.0, 0.0) - jnp.where(normal == 3, 1.0, 0.0)
    flat = jnp.concatenate(
        [
            point_rows, point_rows - step_row, point_rows + step_row,
            point_cols, point_cols - step_col, point_cols + step_col,
            weights_ref[...], jnp.zeros((1, PTS), F32),
        ],
        axis=0,
    )
    tall = flat.T
    cols = jnp.concatenate([tall[:, 3:4], tall[:, 4:5], tall[:, 5:6]], axis=0).astype(jnp.int32)
    wide_rows = jnp.concatenate([flat[0:1], flat[1:2], flat[2:3]], axis=1).astype(jnp.int32)
    wide_cols = jnp.concatenate([flat[3:4], flat[4:5], flat[5:6]], axis=1).astype(jnp.int32)
    weight = jnp.concatenate([weights_ref[...]] * 3, axis=1)
    third = iota((1, 3 * PTS), 1)
    goal = jnp.where(third < PTS, 0.5, jnp.where(third < 2 * PTS, 1.0, 0.0))
    row_hot = jnp.where(iota((ROWS, 3 * PTS), 0) == wide_rows, 1.0, 0.0)

    load_mask.wait()
    load_ahead.wait()
    later = [
        pltpu.make_async_copy(ahead_x_hbm, ahead_x_ref, load_sem.at[2]),
        pltpu.make_async_copy(back_x_hbm.at[pencil], back_x, load_sem.at[3]),
        pltpu.make_async_copy(back_y_hbm, back_y, load_sem.at[4]),
        pltpu.make_async_copy(spread_hbm, spread, load_sem.at[5]),
        pltpu.make_async_copy(target_hbm, target, load_sem.at[6]),
        pltpu.make_async_copy(spread_t_hbm, spread_t, load_sem.at[7]),
    ]
    for load in later:
        load.start()
    line = dot_nt(ahead_ref[...], mask_ref[...].astype(BF16))
    lane8 = iota((8, ROWS), 1)
    cosine, sine = (line[256:264], line[264:272])
    both = jnp.where(lane8 < 64, cosine + pltpu.roll(cosine, 64, 1), sine + pltpu.roll(sine, 64, 1))
    empty = jnp.where(iota((8, ROWS), 0) == 0, both, line[8:16])
    line_ref[...] = jnp.concatenate([line[:8], empty, line[16:256]], axis=0).astype(BF16)

    pl.semaphore_wait(barrier, 53)

    own_lines = lines_ref.at[:, pl.ds(pl.multiple_of(pencil * ROWS, ROWS), ROWS)]

    def line_to(d):
        q = (pencil // 2 + d) % 16
        home = q // 4 * 8 + FIRST + q % 4
        src = line_ref.at[pl.ds(pl.multiple_of(q * 16, 16), 16)]
        return home, remote(src, own_lines, a_send.at[q], a_recv.at[pencil], {"pencil": home})

    def send_line(d):
        home, copy = line_to(d)

        @pl.when(home != pencil)
        def _():
            copy.start()

    each(0, 16, send_line)

    def kz(d, theirs=False):
        other = (pencil + d) % 32
        spot = other if theirs else pencil
        rows = kern.at[tile, spot // 8, spot % 8]
        return remote(rows, rows, kz_send.at[other], kz_recv.at[spot], {"pencil": other})

    each(1, 32, lambda d: kz(d).start())

    @pl.when(owner)
    def _():
        src = line_ref.at[pl.ds(pl.multiple_of((y * 4 + column) * 16, 16), 16)]
        keep = pltpu.make_async_copy(src, own_lines, self_sem)
        keep.start()
        keep.wait()

    across = jnp.broadcast_to(cols, (3 * PTS, 128)) - iota((3 * PTS, 128), 1)
    down = wide_cols - iota((128, 3 * PTS), 0)
    for base in range(0, N, 128):
        at = slice(base, base + 128)
        hot_t_ref[at, :] = jnp.where(down == base, 1.0, 0.0).astype(BF16)
        hot_ref[:, at] = jnp.where(across == base, 1.0, 0.0).astype(BF16)

    each(1, 32, lambda d: kz(d, True).wait_recv())

    def kx(d, theirs=False):
        other = (chip + d) % 4
        spot = other if theirs else chip
        rows = kern.at[spot * 2 + core]
        return remote(rows, rows, kx_send.at[other], kx_recv.at[spot], {"tile": other * 2 + core})

    def kc(d, theirs=False):
        spot = (chip + d) % 4
        rows = kern.at[spot * 2 + (1 - core if theirs else core)]
        return remote(rows, rows, kc_send.at[spot], kc_recv.at[spot], {"tile": chip * 2 + 1 - core})

    each(1, 4, lambda d: kx(d).start())
    kc(0).start()

    def sz(d):
        spot = (mask * 8 + z + d) % 16
        mine = seen.at[y, mask, column]
        where = {"mask": spot // 8, "pencil": y * 8 + spot % 8}
        return remote(mine, mine, sz_send.at[spot], sz_recv.at[mask * 4 + column], where)

    later[0].wait()

    @pl.when(owner)
    def _():
        def line_from(d):
            other = (pencil + d) % 32
            src = line_ref.at[pl.ds(0, 16)]
            dst = lines_ref.at[:, pl.ds(pl.multiple_of(other * ROWS, ROWS), ROWS)]
            return remote(src, dst, a_send.at[0], a_recv.at[other], {"pencil": other})

        each(1, 32, lambda d: line_from(d).wait_recv())
        held = lines_ref[...].astype(F32)
        first = (y == 0) & (column == 0)
        stash = (iota((16, N), 0) == 8) & first
        extra = jnp.where(stash, held, 0.0)
        left = (iota((16, N), 1) % 128) < 64
        cos_sum = jnp.sum(jnp.where(left, extra, 0.0))
        sin_sum = jnp.sum(jnp.where(left, 0.0, extra))
        out = dot_nn(jnp.where(stash, 0.0, held).astype(BF16), ahead_x_ref[...])
        real = out[:8, :KEEP] + out[8:, KEEP:]
        imag = out[8:, :KEEP] - out[:8, KEEP:]
        slot = (sub == 0) & (lane == HALF + 1) & first
        real = jnp.where(slot, cos_sum, real)
        imag = jnp.where(slot, sin_sum, imag)
        still = (sub == 0) & (lane == HALF) & first
        imag = jnp.where(still, real - real.astype(BF16).astype(F32), imag)
        piece = jnp.concatenate([real, imag], axis=0) * (1.0 / (N * N))
        seen[y, mask, column] = piece.astype(BF16)
        each(1, 16, lambda d: sz(d).start())

    def pass_on(d):
        kx(d, True).wait_recv()
        kc(d).start()

    def sz_wait(m, q):
        theirs = seen.at[y, m, q]
        mine = (m == mask) & (q == column)

        @pl.when(jnp.logical_not(mine))
        def _():
            where = {"pencil": y * 8 + (z + 1) % 8}
            remote(theirs, theirs, sz_send.at[q], sz_recv.at[m * 4 + q], where).wait_recv()

    def sy(d, m, q, theirs=False):
        other = (y + d) % 4
        spot = other if theirs else y
        rows = seen.at[spot, m, q]
        return remote(rows, rows, sy_send.at[m, other, q], sy_recv.at[m, spot, q], {"pencil": other * 8 + z})

    def near(i):
        return jnp.where(z < 4, i, 3 - i)

    def forward(m, q):
        sz_wait(m, q)
        each(1, 4, lambda d: sy(d, m, q).start())

    each(0, 4, lambda i: forward(mask, near(i)))
    each(1, 4, pass_on)
    each(0, 4, lambda i: forward(1 - mask, near(3 - i)))
    each(0, 4, lambda d: kc(d, True).wait_recv())

    slot = (sub == 0) & (lane == HALF + 1)
    still = (sub == 0) & (lane == HALF)

    for part in range(8):
        lines = kern[part].astype(F32).reshape(PENCIL, 16, HALF)
        bands[part] = jnp.concatenate(
            [lines[:, :8].reshape(KEEP, HALF), lines[:, 8:].reshape(KEEP, HALF)], axis=1
        )
        middle = bands[part, HALF : HALF + 8]
        rest = middle[1:2, 0:1]
        middle = jnp.where(still, middle + rest, jnp.where((sub == 1) & (lane == 0), 0.0, middle))
        bands[part, HALF : HALF + 8] = middle

    def spectrum(which):
        held = jnp.concatenate([seen[i, which].reshape(64, KEEP) for i in range(4)], axis=0)
        full = dot_nn(pick_ref[...], held)
        real, imag = (full[:KEEP], full[KEEP:])
        mid_real, mid_imag = (real[HALF : HALF + 8], imag[HALF : HALF + 8])
        edge_real = jnp.sum(jnp.where(slot, mid_real, 0.0))
        edge_imag = jnp.sum(jnp.where(slot, mid_imag, 0.0))
        mid_real = jnp.where(slot, pltpu.roll(mid_real, 2, 1), mid_real)
        mid_imag = jnp.where(slot, -pltpu.roll(mid_imag, 2, 1), mid_imag)
        mid_real = jnp.where(still, mid_real + mid_imag, mid_real)
        mid_imag = jnp.where(still, 0.0, mid_imag)
        top_real = jnp.where(sub == 0, edge_real, real[:8])
        top_imag = jnp.where(sub == 0, edge_imag, imag[:8])
        real = jnp.concatenate([top_real, real[8:HALF], mid_real, real[HALF + 8 :]], axis=0)
        imag = jnp.concatenate([top_imag, imag[8:HALF], mid_imag, imag[HALF + 8 :]], axis=0)
        return real, imag

    def remainder(band):
        middle = band[HALF : HALF + 8]
        return (middle - middle.astype(BF16).astype(F32))[0:1, HALF : HALF + 1]

    for load in later[1:]:
        load.wait()
    images = []
    for turn in range(2):
        which = mask if turn == 0 else 1 - mask
        each(0, 12, lambda i, which=which: sy(1 + i // 4, which, i % 4, True).wait_recv())
        real, imag = spectrum(which)
        columned, rests, rests_imag = ([], [], [])
        for k in range(KERN):
            kern_real, kern_imag = (bands[k], bands[KERN + k])
            band_real = kern_real * real - kern_imag * imag
            band_imag = kern_real * imag + kern_imag * real
            band = jnp.concatenate([band_real, band_imag], axis=1).astype(BF16)
            out = dot_nt(back_x[...], band)
            out = jnp.concatenate([out[:ROWS], out[ROWS:]], axis=1)
            rounded = out.astype(BF16)
            columned.append(rounded)
            rest = out - rounded.astype(F32)
            rests.append(rest[:, HALF : HALF + 1] + remainder(band_real))
            rests_imag.append(rest[:, KEEP + HALF : KEEP + HALF + 1] + remainder(band_imag))
        field = dot_nn(jnp.concatenate(columned, axis=0), back_y[...])
        rest_real = jnp.broadcast_to(jnp.concatenate(rests, axis=0), (512, SAMPLES))
        rest_imag = jnp.broadcast_to(jnp.concatenate(rests_imag, axis=0), (512, SAMPLES))
        field = field + jnp.concatenate([rest_real, rest_imag], axis=1)
        if turn == 0:
            fields[...] = field.astype(BF16)
        square = field * field
        square = square[:, :SAMPLES] + square[:, SAMPLES:]
        images.append(square[:128] + square[128:256] + square[256:384] + square[384:])
    image = jnp.concatenate(images, axis=0).astype(BF16)

    loss = jnp.zeros((ROWS, 128), F32)
    picked = jnp.zeros((2 * ROWS, 3 * PTS), F32)
    for base in range(0, N, CHUNK):
        at = slice(base, base + CHUNK)
        fine = dot_nn(image, spread[:, at])
        clear = 0.5 - 0.5 * jnp.tanh(3.0 * fine - 1.5)
        own, other = (clear[:ROWS], clear[ROWS:])
        product = own * other
        union = 1.0 - product
        slope_ref[:, at] = 12.0 * product * (1.0 - own)
        gap = union - target[:, at].astype(F32)
        gap_ref[:, at] = gap
        high = union.astype(BF16)
        rest = (union - high.astype(F32)).astype(BF16)
        picked = picked + dot_nn(jnp.concatenate([high, rest], axis=0), hot_t_ref[at, :])
        square = gap * gap
        loss = loss + (square[:, :128] + square[:, 128:256]) + (square[:, 256:384] + square[:, 384:])
    missed = jnp.sum((picked[:ROWS] + picked[ROWS:]) * row_hot, axis=0, keepdims=True) - goal
    push = weight * missed
    loss = jnp.sum(loss) + jnp.sum(push * missed)
    hits = (row_hot * push).astype(BF16)
    drive = jnp.zeros((ROWS, SAMPLES), F32)
    for base in range(0, N, CHUNK):
        at = slice(base, base + CHUNK)
        pull = gap_ref[:, at] + dot_nn(hits, hot_ref[:, at])
        drive = drive + dot_nn((pull * slope_ref[:, at]).astype(BF16), spread_t[at, :])
    drive = jnp.concatenate([drive, drive], axis=1)
    drive = jnp.concatenate([drive] * KERN, axis=0)
    mixed = (drive * fields[...].astype(F32)).astype(BF16)
    lines = dot_nt(back_y[...], mixed)
    sum_real = jnp.zeros((KEEP, KEEP), F32)
    sum_imag = jnp.zeros((KEEP, KEEP), F32)
    for k in range(KERN):
        at = slice(k * ROWS, (k + 1) * ROWS)
        line = jnp.concatenate([lines[:KEEP, at], lines[KEEP:, at]], axis=1).astype(BF16)
        back = dot_nn(line, back_x[...])
        back_real, back_imag = (back[:, :KEEP], back[:, KEEP:])
        kern_real, kern_imag = (bands[k], bands[KERN + k])
        sum_real = sum_real + (kern_real * back_real + kern_imag * back_imag)
        sum_imag = sum_imag + (kern_real * back_imag - kern_imag * back_real)
    sum_real = sum_real * (2.0 / (N * N))
    sum_imag = sum_imag * (2.0 / (N * N))

    mid_real, mid_imag = (sum_real[HALF : HALF + 8], sum_imag[HALF : HALF + 8])
    turned = dot_nn(jnp.concatenate([mid_real, mid_imag], axis=0).astype(BF16), flip_ref[...])
    edge_real = jnp.sum(jnp.where(still, sum_real[:8], 0.0))
    edge_imag = jnp.sum(jnp.where(still, sum_imag[:8], 0.0))
    fold_real = jnp.where(lane < HALF, mid_real + turned[:8], jnp.where(lane == HALF, mid_real, 0.0))
    fold_imag = jnp.where(lane < HALF, mid_imag - turned[8:], 0.0)
    fold_real = jnp.where(lane == HALF + 1, edge_real, jnp.where(lane == HALF + 2, loss, fold_real))
    fold_imag = jnp.where(lane == HALF + 1, edge_imag, fold_imag)
    mid_real = jnp.where(sub == 0, fold_real, mid_real)
    mid_imag = jnp.where(sub == 0, fold_imag, mid_imag)
    full = jnp.concatenate(
        [
            sum_real[:HALF], mid_real, sum_real[HALF + 8 :],
            sum_imag[:HALF], mid_imag, sum_imag[HALF + 8 :],
        ],
        axis=0,
    ).astype(BF16)
    part_ref[...] = dot_nn(merge_ref[...], full).astype(BF16).reshape(4, 4, 16, KEEP)

    def far(i):
        return near(3 - i)

    def cy(d, q, theirs=False):
        other = (y + d) % 4
        spot = other if theirs else y
        where = {"pencil": other * 8 + z}
        return remote(part_ref.at[other, q], gathered.at[spot, q], cy_send.at[other, q], cy_recv.at[spot, q], where)

    each(0, 12, lambda i: cy(1 + i % 3, far(i // 3)).start())
    gathered[y] = part_ref[y]

    def cz(q):
        home = FIRST + q
        return home, remote(summed.at[q], pieces.at[z], cz_send.at[q], cz_recv.at[z], {"pencil": y * 8 + home})

    def add_piece(i):
        q = far(i)
        each(1, 4, lambda d: cy(d, q, True).wait_recv())
        total = gathered[0, q].astype(F32) + gathered[1, q].astype(F32)
        total = total + (gathered[2, q].astype(F32) + gathered[3, q].astype(F32))
        summed[q] = total.astype(BF16)
        home, copy = cz(q)

        @pl.when(home != z)
        def _():
            copy.start()

    each(0, 4, add_piece)

    def dz(d):
        other = (z + d) % 8
        mine = whole.at[y, column]
        return remote(mine, mine, dz_send.at[other], dz_recv.at[column], {"pencil": y * 8 + other})

    row = iota((16, KEEP), 0)
    lane = iota((16, KEEP), 1)
    note_row = iota((8, 128), 0)
    here = mask * 8 + tile

    def tell(d):
        spot, where = spot_of(d)
        return remote(note, notes.at[here], e_send.at[spot], e_recv.at[here], where)

    def told(d):
        spot, where = spot_of(d)
        return remote(note, notes.at[spot], e_send.at[spot], e_recv.at[spot], where)

    @pl.when(owner)
    def _():
        pieces[z] = summed[column]

        def piece_from(d):
            other = (z + d) % 8
            where = {"pencil": y * 8 + other}
            return remote(summed.at[0], pieces.at[other], cz_send.at[0], cz_recv.at[other], where)

        each(1, 8, lambda d: piece_from(d).wait_recv())
        one = pieces[...].astype(F32)
        one = (one[0] + one[1]) + (one[2] + one[3]) + (one[4] + one[5]) + (one[6] + one[7])
        whole[y, column] = one.astype(BF16)
        each(1, 8, lambda d: dz(d).start())
        first = (y == 0) & (column == 0)
        loss = jnp.sum(jnp.where(first & (row == 0) & (lane == HALF + 2), one, 0.0))
        stash = first & ((row == 0) | (row == 8)) & (lane > HALF + 1)
        center = first & (row == 0) & (lane == HALF)
        energy = jnp.where(stash, 0.0, one * one) * jnp.where(center, 1.0, 0.5)
        energy = jnp.sum(energy)
        note[...] = jnp.where(note_row == 0, energy, jnp.where(note_row == 1, loss, 0.0))
        each(1, 16, lambda d: tell(d).start())
        notes[here] = note[...]

    def dz_wait(q):
        theirs = whole.at[y, q]

        @pl.when(q != column)
        def _():
            where = {"pencil": y * 8 + (z + 1) % 8}
            remote(theirs, theirs, dz_send.at[q], dz_recv.at[q], where).wait_recv()

    def dy(d, q, theirs=False):
        other = (y + d) % 4
        spot = other if theirs else y
        rows = whole.at[spot, q]
        return remote(rows, rows, dy_send.at[other, q], dy_recv.at[spot, q], {"pencil": other * 8 + z})

    def forward_piece(i):
        q = near(i)
        dz_wait(q)
        each(1, 4, lambda d: dy(d, q).start())

    each(0, 4, forward_piece)

    def share(d):
        other = (pencil + d) % 32
        mine = totals.at[y * 4 + column]
        return remote(mine, mine, f_send.at[other], f_recv.at[y * 4 + column], {"pencil": other})

    @pl.when(owner)
    def _():
        each(1, 16, lambda d: told(d).wait_recv())
        total = notes[0]
        for spot in range(1, 16):
            total = total + notes[spot]
        totals[y * 4 + column] = total
        each(1, 32, lambda d: share(d).start())

    each(0, 12, lambda i: dy(1 + i // 4, i % 4, True).wait_recv())

    band = whole[...].astype(F32).reshape(KEEP, KEEP)
    head = band[:16]
    edge_real = jnp.sum(jnp.where((row == 0) & (lane == HALF + 1), head, 0.0))
    edge_imag = jnp.sum(jnp.where((row == 8) & (lane == HALF + 1), head, 0.0))
    head = jnp.where(((row == 0) | (row == 8)) & (lane > HALF), 0.0, head)
    band = jnp.concatenate([head, band[16:]], axis=0)
    pairs = band.reshape(16, 2, 8, KEEP)
    turned = jnp.concatenate([pairs[:, 1:2], -pairs[:, 0:1]], axis=1).reshape(KEEP, KEEP)
    stacked = jnp.concatenate([band, turned], axis=1).astype(BF16)
    lines = dot_nt(back_x[0:ROWS], stacked).astype(BF16)
    for base in range(0, N, CHUNK):
        at = slice(base, base + CHUNK)
        extra = ahead_ref[256:272, at].astype(F32)
        extra = edge_real * extra[0:1] + edge_imag * extra[8:9]
        target[:, at] = (dot_nn(lines, ahead_ref[0:256, at]) + extra).astype(BF16)
    store = pltpu.make_async_copy(target, gradient_hbm, load_sem.at[0])
    store.start()

    each(1, 32, lambda d: kz(d).wait_send())
    each(1, 4, lambda d: kx(d).wait_send())
    each(0, 4, lambda d: kc(d).wait_send())
    each(0, 12, lambda i: sy(1 + i // 4, 0, i % 4).wait_send())
    each(0, 12, lambda i: sy(1 + i // 4, 1, i % 4).wait_send())
    each(0, 12, lambda i: cy(1 + i // 4, i % 4).wait_send())
    each(0, 12, lambda i: dy(1 + i // 4, i % 4).wait_send())

    def sent_line(d):
        home, copy = line_to(d)

        @pl.when(home != pencil)
        def _():
            copy.wait_send()

    each(0, 16, sent_line)

    def sent_piece(q):
        home, copy = cz(q)

        @pl.when(home != z)
        def _():
            copy.wait_send()

    each(0, 4, sent_piece)

    @pl.when(owner)
    def _():
        each(1, 16, lambda d: sz(d).wait_send())
        each(1, 8, lambda d: dz(d).wait_send())

    def share_wait(q):
        theirs = totals.at[q]
        home = q // 4 * 8 + FIRST + q % 4

        @pl.when(home != pencil)
        def _():
            where = {"pencil": (pencil + 1) % 32}
            remote(theirs, theirs, f_send.at[q], f_recv.at[q], where).wait_recv()

    each(0, 16, share_wait)
    total = totals[0]
    for q in range(1, 16):
        total = total + totals[q]
    scale_out[...] = STEP_SIZE * lax.rsqrt(total[0:1] * (1.0 / 16.0) + EPSILON)
    loss_out[0, 0] = jnp.sum(jnp.where(note_row == 1, total, 0.0)) * (0.5 / (128.0 * 8.0 * N * N))
    store.wait()

    @pl.when(owner)
    def _():
        each(1, 16, lambda d: tell(d).wait_send())
        each(1, 32, lambda d: share(d).wait_send())


ANY_SPEC = pl.BlockSpec(memory_space=pl.ANY)
VMEM_SPEC = pl.BlockSpec(memory_space=VMEM)
SMEM_SPEC = pl.BlockSpec(memory_space=pltpu.SMEM)
LIMIT = 56 * 1024 * 1024


def per_device(mask_field, design_target, kernel_spectra, support_radii, edge_points, point_weights):
    table = {name: jnp.asarray(value) for name, value in tables().items()}
    plane = mask_field.reshape(ROWS, N)
    gradient, scale, loss = pl.pallas_call(
        step_kernel,
        out_shape=(
            jax.ShapeDtypeStruct((ROWS, N), BF16),
            jax.ShapeDtypeStruct((1, 128), F32),
            jax.ShapeDtypeStruct((1, 1), F32),
        ),
        in_specs=[ANY_SPEC] * 8 + [VMEM_SPEC] * 6 + [SMEM_SPEC],
        out_specs=(ANY_SPEC, VMEM_SPEC, SMEM_SPEC),
        scratch_shapes=[
            VMEM((ROWS, N), F32),
            VMEM((272, N), BF16),
            VMEM((N, 512), BF16),
            VMEM((256, 512), BF16),
            VMEM((512, 1024), BF16),
            VMEM((SAMPLES, N), BF16),
            VMEM((ROWS, N), BF16),
            VMEM((N, SAMPLES), BF16),
            VMEM((256, ROWS), BF16),
            VMEM((16, N), BF16),
            VMEM((4, 2, 4, 16, KEEP), BF16),
            VMEM((8, 4, 8, 16, HALF), BF16),
            VMEM((8, 16, HALF), BF16),
            VMEM((8, KEEP, KEEP), F32),
            VMEM((512, 1024), BF16),
            VMEM((ROWS, N), F32),
            VMEM((ROWS, N), F32),
            VMEM((3 * PTS, N), BF16),
            VMEM((N, 3 * PTS), BF16),
            VMEM((4, 4, 16, KEEP), BF16),
            VMEM((4, 4, 16, KEEP), BF16),
            VMEM((4, 16, KEEP), BF16),
            VMEM((8, 16, KEEP), BF16),
            VMEM((4, 4, 16, KEEP), BF16),
            VMEM((8, 128), F32),
            VMEM((16, 8, 128), F32),
            VMEM((16, 8, 128), F32),
            DMA((8,)),
            DMA,
        ]
        + [DMA((32,))] * 2
        + [DMA((4,))] * 4
        + [DMA((16,)), DMA((32,)), DMA((16,)), DMA((8,)), DMA((2, 4, 4)), DMA((2, 4, 4))]
        + [DMA((4, 4)), DMA((4, 4)), DMA((4,)), DMA((8,)), DMA((8,)), DMA((4,)), DMA((4, 4)), DMA((4, 4))]
        + [DMA((16,)), DMA((16,)), DMA((32,)), DMA((16,))],
        compiler_params=pltpu.CompilerParams(collective_id=0, has_side_effects=True, vmem_limit_bytes=LIMIT),
        name="step_kernel",
    )(
        plane, table["ahead"], table["ahead_x"], table["back_x"], table["back_y"], table["spread"],
        design_target.reshape(ROWS, N), table["spread_t"], table["pick"], table["merge"], table["flip"],
        kernel_spectra, edge_points.reshape(3, 1, PTS), point_weights, support_radii,
    )
    update = (plane - scale[0, 0] * gradient.astype(F32)).astype(BF16)
    return update.reshape(1, 1, ROWS, N), loss.reshape(())


def solution(mesh):
    placed = (
        P("tile", "mask", "pencil", None),
        P("tile", "pencil", None),
        P(None, None, "pencil", None),
        P(),
        P("tile", None, "pencil"),
        P("tile", "pencil"),
    )
    return jax.shard_map(
        per_device,
        mesh=mesh,
        in_specs=placed,
        out_specs=(P("tile", "mask", "pencil", None), P()),
        check_vma=False,
    )
```

```python
import functools
import math

import jax
import jax.numpy as jnp
import numpy as np
from jax import lax
from jax.experimental import pallas as pl
from jax.experimental.pallas import tpu as pltpu
from jax.sharding import PartitionSpec as P
from ml_dtypes import bfloat16

N = 4096
KEEP = 256
HALF = 128
KERN = 4
ROWS = 128
SAMPLES = 512
PENCIL = 32
CHUNK = 512
PTS = 256
FIRST = 2
EPSILON = 1e-06
STEP_SIZE = 0.2
F32 = jnp.float32
BF16 = jnp.bfloat16
MESH = pl.DeviceIdType.MESH
VMEM = pltpu.VMEM
DMA = pltpu.SemaphoreType.DMA


def angles(first, second, period):
    return 2.0 * np.pi / period * ((first[:, None] * second[None, :]) % period)


@functools.cache
def tables():
    pixels = np.arange(N)
    freqs = np.arange(KEEP) - HALF
    half = np.arange(136)
    theta = angles(half, pixels, N)
    theta_cos, theta_sin = (np.cos(theta), np.sin(theta))
    theta_cos[129:], theta_sin[129:] = (0.0, 0.0)
    ahead = np.stack([theta_cos.reshape(17, 8, N), -theta_sin.reshape(17, 8, N)], axis=1).reshape(272, N)
    theta = angles(pixels, freqs, N)
    ahead_x = np.concatenate([np.cos(theta), np.sin(theta)], axis=1)
    theta_cos, theta_sin = (np.cos(theta), np.sin(theta))
    back_x = np.concatenate(
        [
            np.concatenate([theta_cos, -theta_sin], axis=1).reshape(PENCIL, ROWS, 512),
            np.concatenate([theta_sin, theta_cos], axis=1).reshape(PENCIL, ROWS, 512),
        ],
        axis=1,
    )
    theta = angles(np.abs(freqs), np.arange(SAMPLES), SAMPLES)
    sign = np.where(freqs < 0, -1.0, 1.0)[:, None]
    back_y = np.concatenate(
        [
            np.concatenate([np.cos(theta), sign * np.sin(theta)], axis=1),
            np.concatenate([-np.sin(theta), sign * np.cos(theta)], axis=1),
        ],
        axis=0,
    )
    shift = np.arange(N)
    bell = np.ones(N)
    for freq in range(1, 256):
        bell += 2.0 * np.cos(2.0 * np.pi / N * ((freq * shift) % N))
    bell /= SAMPLES
    bell += np.cos(2.0 * np.pi / N * ((256 * shift) % N)) / SAMPLES
    spread = bell[(pixels[None, :] - 8 * np.arange(SAMPLES)[:, None]) % N]
    pick = np.zeros((512, 256))
    for row in range(KEEP):
        a = abs(row - HALF)
        if a < HALF:
            pick[row, 16 * (a // 8) + a % 8] = 1.0
            pick[KEEP + row, 16 * (a // 8) + 8 + a % 8] = 1.0
    flip = np.zeros((KEEP, KEEP))
    for lane in range(1, KEEP):
        flip[KEEP - lane, lane] = 1.0
    return {
        "ahead": ahead.astype(bfloat16),
        "ahead_x": ahead_x.astype(bfloat16),
        "back_x": back_x.astype(bfloat16),
        "back_y": back_y.astype(bfloat16),
        "spread": spread.astype(bfloat16),
        "spread_t": np.ascontiguousarray(spread.T).astype(bfloat16),
        "pick": pick.astype(bfloat16),
        "merge": np.ascontiguousarray(pick.T).astype(bfloat16),
        "flip": flip.astype(bfloat16),
    }


def dot_nn(left, right):
    return lax.dot_general(left, right, (((1,), (0,)), ((), ())), preferred_element_type=F32)


def dot_nt(left, right):
    return lax.dot_general(left, right, (((1,), (1,)), ((), ())), preferred_element_type=F32)


def iota(shape, axis):
    return lax.broadcasted_iota(jnp.int32, shape, axis)


def each(low, high, body):
    def step(i, carry):
        body(i)
        return carry

    lax.fori_loop(low, high, step, 0)


def place():
    tile = lax.axis_index("tile")
    mask = lax.axis_index("mask")
    pencil = lax.axis_index("pencil")
    return tile, mask, pencil, pencil // 8, pencil % 8


def remote(src, dst, send, recv, where):
    return pltpu.make_async_remote_copy(
        src_ref=src, dst_ref=dst, send_sem=send, recv_sem=recv, device_id=where, device_id_type=MESH
    )


def step_kernel(
    mask_hbm, ahead_hbm, ahead_x_hbm, back_x_hbm, back_y_hbm, spread_hbm, target_hbm, spread_t_hbm,
    pick_ref, merge_ref, flip_ref, spectra_ref, points_ref, weights_ref, radii_ref,
    gradient_hbm, scale_out, loss_out,
    mask_ref, ahead_ref, ahead_x_ref, back_x, back_y, spread, target, spread_t,
    line_ref, lines_ref, seen, kern, slices, bands, fields, gap_ref, slope_ref, hot_ref, hot_t_ref,
    part_ref, gathered, summed, pieces, whole, note, notes, totals,
    load_sem, self_sem, kz_send, kz_recv, ka_send, ka_recv, kb_send, kb_recv, kd_send, kd_recv, ke_send, ke_recv, kc_send, kc_recv,
    a_send, a_recv, sz_send, sz_recv, sy_send, sy_recv,
    cy_send, cy_recv, cz_send, cz_recv, dz_send, dz_recv, dy_send, dy_recv, e_send, e_recv, f_send, f_recv,
):
    tile, mask, pencil, y, z = place()
    chip, core = (tile // 2, tile % 2)
    owner = (z >= FIRST) & (z < FIRST + 4)
    column = z - FIRST
    load_mask = pltpu.make_async_copy(mask_hbm, mask_ref, load_sem.at[0])
    load_ahead = pltpu.make_async_copy(ahead_hbm, ahead_ref, load_sem.at[1])
    load_mask.start()
    load_ahead.start()
    barrier = pltpu.get_barrier_semaphore()

    def greet(where):
        pl.semaphore_signal(barrier, inc=1, device_id=where, device_id_type=MESH)

    def spot_of(d):
        spot = (mask * 8 + tile + d) % 16
        return spot, {"mask": spot // 8, "tile": spot % 8}

    each(1, 32, lambda d: greet({"pencil": (pencil + d) % 32}))
    each(1, 16, lambda d: greet(spot_of(d)[1]))
    each(1, 8, lambda d: greet({"mask": 1 - mask, "pencil": y * 8 + (z + d) % 8}))

    sub = iota((8, KEEP), 0)
    lane = iota((8, KEEP), 1)
    freq_u = lane - HALF
    freq_v = sub + pencil * 8 - HALF
    radius = freq_u * freq_u + freq_v * freq_v
    parts = []
    for c in range(2):
        for k in range(KERN):
            limit = radii_ref[k] * radii_ref[k]
            parts.append(jnp.where(radius <= limit, spectra_ref[c, k], 0.0))
    plain = jnp.concatenate(parts, axis=0)
    turned = dot_nn(plain.astype(BF16), flip_ref[...])
    sign = jnp.where(iota((64, KEEP), 0) < 32, 1.0, -1.0)
    low = jnp.where(pencil < 16, 1.0, 0.0).astype(F32)
    plain = low * (turned * sign) + (1.0 - low) * plain
    spare = (sub == 1) & (lane == 0) & (pencil == 16)
    for part in range(8):
        rows = plain[part * 8 : part * 8 + 8]
        rest = rows - rows.astype(BF16).astype(F32)
        rows = jnp.where(spare, rest[0:1, HALF : HALF + 1], rows)
        slices[part] = jnp.concatenate([rows[:, :HALF], rows[:, HALF:]], axis=0).astype(BF16)
    kern[core, chip, y, z] = slices[tile]

    point_rows = points_ref[0].astype(F32) - (pencil * ROWS).astype(F32)
    point_cols = points_ref[1].astype(F32)
    normal = points_ref[2]
    step_row = jnp.where(normal == 0, 1.0, 0.0) - jnp.where(normal == 1, 1.0, 0.0)
    step_col = jnp.where(normal == 2, 1.0, 0.0) - jnp.where(normal == 3, 1.0, 0.0)
    flat = jnp.concatenate(
        [
            point_rows, point_rows - step_row, point_rows + step_row,
            point_cols, point_cols - step_col, point_cols + step_col,
            weights_ref[...], jnp.zeros((1, PTS), F32),
        ],
        axis=0,
    )
    tall = flat.T
    cols = jnp.concatenate([tall[:, 3:4], tall[:, 4:5], tall[:, 5:6]], axis=0).astype(jnp.int32)
    wide_rows = jnp.concatenate([flat[0:1], flat[1:2], flat[2:3]], axis=1).astype(jnp.int32)
    wide_cols = jnp.concatenate([flat[3:4], flat[4:5], flat[5:6]], axis=1).astype(jnp.int32)
    weight = jnp.concatenate([weights_ref[...]] * 3, axis=1)
    third = iota((1, 3 * PTS), 1)
    goal = jnp.where(third < PTS, 0.5, jnp.where(third < 2 * PTS, 1.0, 0.0))
    row_hot = jnp.where(iota((ROWS, 3 * PTS), 0) == wide_rows, 1.0, 0.0)

    load_mask.wait()
    load_ahead.wait()
    later = [
        pltpu.make_async_copy(ahead_x_hbm, ahead_x_ref, load_sem.at[2]),
        pltpu.make_async_copy(back_x_hbm.at[pencil], back_x, load_sem.at[3]),
        pltpu.make_async_copy(back_y_hbm, back_y, load_sem.at[4]),
        pltpu.make_async_copy(spread_hbm, spread, load_sem.at[5]),
        pltpu.make_async_copy(target_hbm, target, load_sem.at[6]),
        pltpu.make_async_copy(spread_t_hbm, spread_t, load_sem.at[7]),
    ]
    for load in later:
        load.start()
    line = dot_nt(ahead_ref[...], mask_ref[...].astype(BF16))
    lane8 = iota((8, ROWS), 1)
    cosine, sine = (line[256:264], line[264:272])
    both = jnp.where(lane8 < 64, cosine + pltpu.roll(cosine, 64, 1), sine + pltpu.roll(sine, 64, 1))
    empty = jnp.where(iota((8, ROWS), 0) == 0, both, line[8:16])
    line_ref[...] = jnp.concatenate([line[:8], empty, line[16:256]], axis=0).astype(BF16)

    pl.semaphore_wait(barrier, 53)

    def hop(rows, send, recv, other, spot, where):
        return remote(rows, rows, send.at[other], recv.at[spot], where)

    def kz(d, theirs=False):
        other = (z + d) % 8
        spot = other if theirs else z
        return hop(kern.at[core, chip, y, spot], kz_send, kz_recv, other, spot, {"pencil": y * 8 + other})

    def along_x(d, theirs):
        other = (chip + d) % 4
        return other, other if theirs else chip, {"tile": other * 2 + core}

    def along_y(d, theirs):
        other = (y + d) % 4
        return other, other if theirs else y, {"pencil": other * 8 + z}

    def ka(d, theirs=False):
        other, spot, where = along_x(d, theirs)
        return hop(kern.at[core, spot, y, pl.ds(0, 4)], ka_send, ka_recv, other, spot, where)

    def kb(d, theirs=False):
        other, spot, where = along_y(d, theirs)
        return hop(kern.at[core, chip, spot, pl.ds(4, 4)], kb_send, kb_recv, other, spot, where)

    def kd(d, theirs=False):
        other, spot, where = along_y(d, theirs)
        return hop(kern.at[core, pl.ds(0, 4), spot, pl.ds(0, 4)], kd_send, kd_recv, other, spot, where)

    def ke(d, theirs=False):
        other, spot, where = along_x(d, theirs)
        return hop(kern.at[core, spot, pl.ds(0, 4), pl.ds(4, 4)], ke_send, ke_recv, other, spot, where)

    def kc(half, theirs=False):
        side = 1 - core if theirs else core
        rows = kern.at[side, pl.ds(0, 4), pl.ds(0, 4), pl.ds(4 * half, 4)]
        return remote(rows, rows, kc_send.at[half], kc_recv.at[half], {"tile": chip * 2 + 1 - core})

    each(1, 8, lambda d: kz(d).start())

    own_lines = lines_ref.at[:, pl.ds(pl.multiple_of(pencil * ROWS, ROWS), ROWS)]

    def line_to(d):
        q = (pencil // 2 + d) % 16
        home = q // 4 * 8 + FIRST + q % 4
        src = line_ref.at[pl.ds(pl.multiple_of(q * 16, 16), 16)]
        return home, remote(src, own_lines, a_send.at[q], a_recv.at[pencil], {"pencil": home})

    def send_line(d):
        home, copy = line_to(d)

        @pl.when(home != pencil)
        def _():
            copy.start()

    each(0, 16, send_line)

    @pl.when(owner)
    def _():
        src = line_ref.at[pl.ds(pl.multiple_of((y * 4 + column) * 16, 16), 16)]
        keep = pltpu.make_async_copy(src, own_lines, self_sem)
        keep.start()
        keep.wait()

    each(1, 8, lambda d: kz(d, True).wait_recv())
    each(1, 4, lambda d: ka(d).start())
    each(1, 4, lambda d: kb(d).start())

    down = wide_cols - iota((128, 3 * PTS), 0)
    for base in range(0, N, 128):
        hot_t_ref[base : base + 128, :] = jnp.where(down == base, 1.0, 0.0).astype(BF16)

    each(1, 4, lambda d: ka(d, True).wait_recv())
    each(1, 4, lambda d: kd(d).start())
    each(1, 4, lambda d: kb(d, True).wait_recv())
    each(1, 4, lambda d: ke(d).start())

    def sz(d):
        spot = (mask * 8 + z + d) % 16
        mine = seen.at[y, mask, column]
        where = {"mask": spot // 8, "pencil": y * 8 + spot % 8}
        return remote(mine, mine, sz_send.at[spot], sz_recv.at[mask * 4 + column], where)

    later[0].wait()

    @pl.when(owner)
    def _():
        def line_from(d):
            other = (pencil + d) % 32
            src = line_ref.at[pl.ds(0, 16)]
            dst = lines_ref.at[:, pl.ds(pl.multiple_of(other * ROWS, ROWS), ROWS)]
            return remote(src, dst, a_send.at[0], a_recv.at[other], {"pencil": other})

        each(1, 32, lambda d: line_from(d).wait_recv())
        held = lines_ref[...].astype(F32)
        first = (y == 0) & (column == 0)
        stash = (iota((16, N), 0) == 8) & first
        extra = jnp.where(stash, held, 0.0)
        left = (iota((16, N), 1) % 128) < 64
        cos_sum = jnp.sum(jnp.where(left, extra, 0.0))
        sin_sum = jnp.sum(jnp.where(left, 0.0, extra))
        out = dot_nn(jnp.where(stash, 0.0, held).astype(BF16), ahead_x_ref[...])
        real = out[:8, :KEEP] + out[8:, KEEP:]
        imag = out[8:, :KEEP] - out[:8, KEEP:]
        slot = (sub == 0) & (lane == HALF + 1) & first
        real = jnp.where(slot, cos_sum, real)
        imag = jnp.where(slot, sin_sum, imag)
        still = (sub == 0) & (lane == HALF) & first
        imag = jnp.where(still, real - real.astype(BF16).astype(F32), imag)
        piece = jnp.concatenate([real, imag], axis=0) * (1.0 / (N * N))
        seen[y, mask, column] = piece.astype(BF16)
        each(1, 16, lambda d: sz(d).start())

    across = jnp.broadcast_to(cols, (3 * PTS, 128)) - iota((3 * PTS, 128), 1)
    for base in range(0, N, 128):
        hot_ref[:, base : base + 128] = jnp.where(across == base, 1.0, 0.0).astype(BF16)

    each(1, 4, lambda d: kd(d, True).wait_recv())
    kc(0).start()
    each(1, 4, lambda d: ke(d, True).wait_recv())
    kc(1).start()

    def sz_wait(m, q):
        theirs = seen.at[y, m, q]
        mine = (m == mask) & (q == column)

        @pl.when(jnp.logical_not(mine))
        def _():
            where = {"pencil": y * 8 + (z + 1) % 8}
            remote(theirs, theirs, sz_send.at[q], sz_recv.at[m * 4 + q], where).wait_recv()

    def sy(d, m, q, theirs=False):
        other = (y + d) % 4
        spot = other if theirs else y
        rows = seen.at[spot, m, q]
        return remote(rows, rows, sy_send.at[m, other, q], sy_recv.at[m, spot, q], {"pencil": other * 8 + z})

    def near(i):
        return jnp.where(z < 4, i, 3 - i)

    def forward(m, q):
        sz_wait(m, q)
        each(1, 4, lambda d: sy(d, m, q).start())

    each(0, 4, lambda i: forward(mask, near(i)))
    each(0, 4, lambda i: forward(1 - mask, near(3 - i)))
    kc(0, True).wait_recv()
    kc(1, True).wait_recv()

    slot = (sub == 0) & (lane == HALF + 1)
    still = (sub == 0) & (lane == HALF)

    for part in range(8):
        lines = kern[part % 2, part // 2].astype(F32).reshape(PENCIL, 16, HALF)
        bands[part] = jnp.concatenate(
            [lines[:, :8].reshape(KEEP, HALF), lines[:, 8:].reshape(KEEP, HALF)], axis=1
        )
        middle = bands[part, HALF : HALF + 8]
        rest = middle[1:2, 0:1]
        middle = jnp.where(still, middle + rest, jnp.where((sub == 1) & (lane == 0), 0.0, middle))
        bands[part, HALF : HALF + 8] = middle

    def spectrum(which):
        held = jnp.concatenate([seen[i, which].reshape(64, KEEP) for i in range(4)], axis=0)
        full = dot_nn(pick_ref[...], held)
        real, imag = (full[:KEEP], full[KEEP:])
        mid_real, mid_imag = (real[HALF : HALF + 8], imag[HALF : HALF + 8])
        edge_real = jnp.sum(jnp.where(slot, mid_real, 0.0))
        edge_imag = jnp.sum(jnp.where(slot, mid_imag, 0.0))
        mid_real = jnp.where(slot, pltpu.roll(mid_real, 2, 1), mid_real)
        mid_imag = jnp.where(slot, -pltpu.roll(mid_imag, 2, 1), mid_imag)
        mid_real = jnp.where(still, mid_real + mid_imag, mid_real)
        mid_imag = jnp.where(still, 0.0, mid_imag)
        top_real = jnp.where(sub == 0, edge_real, real[:8])
        top_imag = jnp.where(sub == 0, edge_imag, imag[:8])
        real = jnp.concatenate([top_real, real[8:HALF], mid_real, real[HALF + 8 :]], axis=0)
        imag = jnp.concatenate([top_imag, imag[8:HALF], mid_imag, imag[HALF + 8 :]], axis=0)
        return real, imag

    def remainder(band):
        middle = band[HALF : HALF + 8]
        return (middle - middle.astype(BF16).astype(F32))[0:1, HALF : HALF + 1]

    for load in later[1:]:
        load.wait()
    images = []
    for turn in range(2):
        which = mask if turn == 0 else 1 - mask
        each(0, 12, lambda i, which=which: sy(1 + i // 4, which, i % 4, True).wait_recv())
        real, imag = spectrum(which)
        columned, rests, rests_imag = ([], [], [])
        for k in range(KERN):
            kern_real, kern_imag = (bands[k], bands[KERN + k])
            band_real = kern_real * real - kern_imag * imag
            band_imag = kern_real * imag + kern_imag * real
            band = jnp.concatenate([band_real, band_imag], axis=1).astype(BF16)
            out = dot_nt(back_x[...], band)
            out = jnp.concatenate([out[:ROWS], out[ROWS:]], axis=1)
            rounded = out.astype(BF16)
            columned.append(rounded)
            rest = out - rounded.astype(F32)
            rests.append(rest[:, HALF : HALF + 1] + remainder(band_real))
            rests_imag.append(rest[:, KEEP + HALF : KEEP + HALF + 1] + remainder(band_imag))
        field = dot_nn(jnp.concatenate(columned, axis=0), back_y[...])
        rest_real = jnp.broadcast_to(jnp.concatenate(rests, axis=0), (512, SAMPLES))
        rest_imag = jnp.broadcast_to(jnp.concatenate(rests_imag, axis=0), (512, SAMPLES))
        field = field + jnp.concatenate([rest_real, rest_imag], axis=1)
        if turn == 0:
            fields[...] = field.astype(BF16)
        square = field * field
        square = square[:, :SAMPLES] + square[:, SAMPLES:]
        images.append(square[:128] + square[128:256] + square[256:384] + square[384:])
    image = jnp.concatenate(images, axis=0).astype(BF16)

    loss = jnp.zeros((ROWS, 128), F32)
    picked = jnp.zeros((2 * ROWS, 3 * PTS), F32)
    for base in range(0, N, CHUNK):
        at = slice(base, base + CHUNK)
        fine = dot_nn(image, spread[:, at])
        clear = 0.5 - 0.5 * jnp.tanh(3.0 * fine - 1.5)
        own, other = (clear[:ROWS], clear[ROWS:])
        product = own * other
        union = 1.0 - product
        slope_ref[:, at] = 12.0 * product * (1.0 - own)
        gap = union - target[:, at].astype(F32)
        gap_ref[:, at] = gap
        high = union.astype(BF16)
        rest = (union - high.astype(F32)).astype(BF16)
        picked = picked + dot_nn(jnp.concatenate([high, rest], axis=0), hot_t_ref[at, :])
        square = gap * gap
        loss = loss + (square[:, :128] + square[:, 128:256]) + (square[:, 256:384] + square[:, 384:])
    missed = jnp.sum((picked[:ROWS] + picked[ROWS:]) * row_hot, axis=0, keepdims=True) - goal
    push = weight * missed
    loss = jnp.sum(loss) + jnp.sum(push * missed)
    hits = (row_hot * push).astype(BF16)
    drive = jnp.zeros((ROWS, SAMPLES), F32)
    for base in range(0, N, CHUNK):
        at = slice(base, base + CHUNK)
        pull = gap_ref[:, at] + dot_nn(hits, hot_ref[:, at])
        drive = drive + dot_nn((pull * slope_ref[:, at]).astype(BF16), spread_t[at, :])
    drive = jnp.concatenate([drive, drive], axis=1)
    drive = jnp.concatenate([drive] * KERN, axis=0)
    mixed = (drive * fields[...].astype(F32)).astype(BF16)
    lines = dot_nt(back_y[...], mixed)
    sum_real = jnp.zeros((KEEP, KEEP), F32)
    sum_imag = jnp.zeros((KEEP, KEEP), F32)
    for k in range(KERN):
        at = slice(k * ROWS, (k + 1) * ROWS)
        line = jnp.concatenate([lines[:KEEP, at], lines[KEEP:, at]], axis=1).astype(BF16)
        back = dot_nn(line, back_x[...])
        back_real, back_imag = (back[:, :KEEP], back[:, KEEP:])
        kern_real, kern_imag = (bands[k], bands[KERN + k])
        sum_real = sum_real + (kern_real * back_real + kern_imag * back_imag)
        sum_imag = sum_imag + (kern_real * back_imag - kern_imag * back_real)
    sum_real = sum_real * (2.0 / (N * N))
    sum_imag = sum_imag * (2.0 / (N * N))

    mid_real, mid_imag = (sum_real[HALF : HALF + 8], sum_imag[HALF : HALF + 8])
    turned = dot_nn(jnp.concatenate([mid_real, mid_imag], axis=0).astype(BF16), flip_ref[...])
    edge_real = jnp.sum(jnp.where(still, sum_real[:8], 0.0))
    edge_imag = jnp.sum(jnp.where(still, sum_imag[:8], 0.0))
    fold_real = jnp.where(lane < HALF, mid_real + turned[:8], jnp.where(lane == HALF, mid_real, 0.0))
    fold_imag = jnp.where(lane < HALF, mid_imag - turned[8:], 0.0)
    fold_real = jnp.where(lane == HALF + 1, edge_real, jnp.where(lane == HALF + 2, loss, fold_real))
    fold_imag = jnp.where(lane == HALF + 1, edge_imag, fold_imag)
    mid_real = jnp.where(sub == 0, fold_real, mid_real)
    mid_imag = jnp.where(sub == 0, fold_imag, mid_imag)
    full = jnp.concatenate(
        [
            sum_real[:HALF], mid_real, sum_real[HALF + 8 :],
            sum_imag[:HALF], mid_imag, sum_imag[HALF + 8 :],
        ],
        axis=0,
    ).astype(BF16)
    part_ref[...] = dot_nn(merge_ref[...], full).astype(BF16).reshape(4, 4, 16, KEEP)

    def far(i):
        return near(3 - i)

    def cy(d, q, theirs=False):
        other = (y + d) % 4
        spot = other if theirs else y
        where = {"pencil": other * 8 + z}
        return remote(part_ref.at[other, q], gathered.at[spot, q], cy_send.at[other, q], cy_recv.at[spot, q], where)

    each(0, 12, lambda i: cy(1 + i % 3, far(i // 3)).start())
    gathered[y] = part_ref[y]

    def cz(q):
        home = FIRST + q
        return home, remote(summed.at[q], pieces.at[z], cz_send.at[q], cz_recv.at[z], {"pencil": y * 8 + home})

    def add_piece(i):
        q = far(i)
        each(1, 4, lambda d: cy(d, q, True).wait_recv())
        total = gathered[0, q].astype(F32) + gathered[1, q].astype(F32)
        total = total + (gathered[2, q].astype(F32) + gathered[3, q].astype(F32))
        summed[q] = total.astype(BF16)
        home, copy = cz(q)

        @pl.when(home != z)
        def _():
            copy.start()

    each(0, 4, add_piece)

    def dz(d):
        other = (z + d) % 8
        mine = whole.at[y, column]
        return remote(mine, mine, dz_send.at[other], dz_recv.at[column], {"pencil": y * 8 + other})

    row = iota((16, KEEP), 0)
    lane = iota((16, KEEP), 1)
    note_row = iota((8, 128), 0)
    here = mask * 8 + tile

    def tell(d):
        spot, where = spot_of(d)
        return remote(note, notes.at[here], e_send.at[spot], e_recv.at[here], where)

    def told(d):
        spot, where = spot_of(d)
        return remote(note, notes.at[spot], e_send.at[spot], e_recv.at[spot], where)

    @pl.when(owner)
    def _():
        pieces[z] = summed[column]

        def piece_from(d):
            other = (z + d) % 8
            where = {"pencil": y * 8 + other}
            return remote(summed.at[0], pieces.at[other], cz_send.at[0], cz_recv.at[other], where)

        each(1, 8, lambda d: piece_from(d).wait_recv())
        one = pieces[...].astype(F32)
        one = (one[0] + one[1]) + (one[2] + one[3]) + (one[4] + one[5]) + (one[6] + one[7])
        whole[y, column] = one.astype(BF16)
        each(1, 8, lambda d: dz(d).start())
        first = (y == 0) & (column == 0)
        loss = jnp.sum(jnp.where(first & (row == 0) & (lane == HALF + 2), one, 0.0))
        stash = first & ((row == 0) | (row == 8)) & (lane > HALF + 1)
        center = first & (row == 0) & (lane == HALF)
        energy = jnp.where(stash, 0.0, one * one) * jnp.where(center, 1.0, 0.5)
        energy = jnp.sum(energy)
        note[...] = jnp.where(note_row == 0, energy, jnp.where(note_row == 1, loss, 0.0))
        each(1, 16, lambda d: tell(d).start())
        notes[here] = note[...]

    def dz_wait(q):
        theirs = whole.at[y, q]

        @pl.when(q != column)
        def _():
            where = {"pencil": y * 8 + (z + 1) % 8}
            remote(theirs, theirs, dz_send.at[q], dz_recv.at[q], where).wait_recv()

    def dy(d, q, theirs=False):
        other = (y + d) % 4
        spot = other if theirs else y
        rows = whole.at[spot, q]
        return remote(rows, rows, dy_send.at[other, q], dy_recv.at[spot, q], {"pencil": other * 8 + z})

    def forward_piece(i):
        q = near(i)
        dz_wait(q)
        each(1, 4, lambda d: dy(d, q).start())

    each(0, 4, forward_piece)

    def share(d):
        other = (pencil + d) % 32
        mine = totals.at[y * 4 + column]
        return remote(mine, mine, f_send.at[other], f_recv.at[y * 4 + column], {"pencil": other})

    @pl.when(owner)
    def _():
        each(1, 16, lambda d: told(d).wait_recv())
        total = notes[0]
        for spot in range(1, 16):
            total = total + notes[spot]
        totals[y * 4 + column] = total
        each(1, 32, lambda d: share(d).start())

    each(0, 12, lambda i: dy(1 + i // 4, i % 4, True).wait_recv())

    band = whole[...].astype(F32).reshape(KEEP, KEEP)
    head = band[:16]
    edge_real = jnp.sum(jnp.where((row == 0) & (lane == HALF + 1), head, 0.0))
    edge_imag = jnp.sum(jnp.where((row == 8) & (lane == HALF + 1), head, 0.0))
    head = jnp.where(((row == 0) | (row == 8)) & (lane > HALF), 0.0, head)
    band = jnp.concatenate([head, band[16:]], axis=0)
    pairs = band.reshape(16, 2, 8, KEEP)
    turned = jnp.concatenate([pairs[:, 1:2], -pairs[:, 0:1]], axis=1).reshape(KEEP, KEEP)
    stacked = jnp.concatenate([band, turned], axis=1).astype(BF16)
    lines = dot_nt(back_x[0:ROWS], stacked).astype(BF16)
    for base in range(0, N, CHUNK):
        at = slice(base, base + CHUNK)
        extra = ahead_ref[256:272, at].astype(F32)
        extra = edge_real * extra[0:1] + edge_imag * extra[8:9]
        target[:, at] = (dot_nn(lines, ahead_ref[0:256, at]) + extra).astype(BF16)
    store = pltpu.make_async_copy(target, gradient_hbm, load_sem.at[0])
    store.start()

    each(1, 8, lambda d: kz(d).wait_send())
    for step in (ka, kb, kd, ke):
        each(1, 4, lambda d, step=step: step(d).wait_send())
    kc(0).wait_send()
    kc(1).wait_send()
    each(0, 12, lambda i: sy(1 + i // 4, 0, i % 4).wait_send())
    each(0, 12, lambda i: sy(1 + i // 4, 1, i % 4).wait_send())
    each(0, 12, lambda i: cy(1 + i // 4, i % 4).wait_send())
    each(0, 12, lambda i: dy(1 + i // 4, i % 4).wait_send())

    def sent_line(d):
        home, copy = line_to(d)

        @pl.when(home != pencil)
        def _():
            copy.wait_send()

    each(0, 16, sent_line)

    def sent_piece(q):
        home, copy = cz(q)

        @pl.when(home != z)
        def _():
            copy.wait_send()

    each(0, 4, sent_piece)

    @pl.when(owner)
    def _():
        each(1, 16, lambda d: sz(d).wait_send())
        each(1, 8, lambda d: dz(d).wait_send())

    def share_wait(q):
        theirs = totals.at[q]
        home = q // 4 * 8 + FIRST + q % 4

        @pl.when(home != pencil)
        def _():
            where = {"pencil": (pencil + 1) % 32}
            remote(theirs, theirs, f_send.at[q], f_recv.at[q], where).wait_recv()

    each(0, 16, share_wait)
    total = totals[0]
    for q in range(1, 16):
        total = total + totals[q]
    scale_out[...] = STEP_SIZE * lax.rsqrt(total[0:1] * (1.0 / 16.0) + EPSILON)
    loss_out[0, 0] = jnp.sum(jnp.where(note_row == 1, total, 0.0)) * (0.5 / (128.0 * 8.0 * N * N))
    store.wait()

    @pl.when(owner)
    def _():
        each(1, 16, lambda d: tell(d).wait_send())
        each(1, 32, lambda d: share(d).wait_send())


ANY_SPEC = pl.BlockSpec(memory_space=pl.ANY)
VMEM_SPEC = pl.BlockSpec(memory_space=VMEM)
SMEM_SPEC = pl.BlockSpec(memory_space=pltpu.SMEM)
LIMIT = 56 * 1024 * 1024


def per_device(mask_field, design_target, kernel_spectra, support_radii, edge_points, point_weights):
    table = {name: jnp.asarray(value) for name, value in tables().items()}
    plane = mask_field.reshape(ROWS, N)
    gradient, scale, loss = pl.pallas_call(
        step_kernel,
        out_shape=(
            jax.ShapeDtypeStruct((ROWS, N), BF16),
            jax.ShapeDtypeStruct((1, 128), F32),
            jax.ShapeDtypeStruct((1, 1), F32),
        ),
        in_specs=[ANY_SPEC] * 8 + [VMEM_SPEC] * 6 + [SMEM_SPEC],
        out_specs=(ANY_SPEC, VMEM_SPEC, SMEM_SPEC),
        scratch_shapes=[
            VMEM((ROWS, N), F32),
            VMEM((272, N), BF16),
            VMEM((N, 512), BF16),
            VMEM((256, 512), BF16),
            VMEM((512, 1024), BF16),
            VMEM((SAMPLES, N), BF16),
            VMEM((ROWS, N), BF16),
            VMEM((N, SAMPLES), BF16),
            VMEM((256, ROWS), BF16),
            VMEM((16, N), BF16),
            VMEM((4, 2, 4, 16, KEEP), BF16),
            VMEM((2, 4, 4, 8, 16, HALF), BF16),
            VMEM((8, 16, HALF), BF16),
            VMEM((8, KEEP, KEEP), F32),
            VMEM((512, 1024), BF16),
            VMEM((ROWS, N), F32),
            VMEM((ROWS, N), F32),
            VMEM((3 * PTS, N), BF16),
            VMEM((N, 3 * PTS), BF16),
            VMEM((4, 4, 16, KEEP), BF16),
            VMEM((4, 4, 16, KEEP), BF16),
            VMEM((4, 16, KEEP), BF16),
            VMEM((8, 16, KEEP), BF16),
            VMEM((4, 4, 16, KEEP), BF16),
            VMEM((8, 128), F32),
            VMEM((16, 8, 128), F32),
            VMEM((16, 8, 128), F32),
            DMA((8,)),
            DMA,
        ]
        + [DMA((8,))] * 2
        + [DMA((4,))] * 8
        + [DMA((2,))] * 2
        + [DMA((16,)), DMA((32,)), DMA((16,)), DMA((8,)), DMA((2, 4, 4)), DMA((2, 4, 4))]
        + [DMA((4, 4)), DMA((4, 4)), DMA((4,)), DMA((8,)), DMA((8,)), DMA((4,)), DMA((4, 4)), DMA((4, 4))]
        + [DMA((16,)), DMA((16,)), DMA((32,)), DMA((16,))],
        compiler_params=pltpu.CompilerParams(collective_id=0, has_side_effects=True, vmem_limit_bytes=LIMIT),
        name="step_kernel",
    )(
        plane, table["ahead"], table["ahead_x"], table["back_x"], table["back_y"], table["spread"],
        design_target.reshape(ROWS, N), table["spread_t"], table["pick"], table["merge"], table["flip"],
        kernel_spectra, edge_points.reshape(3, 1, PTS), point_weights, support_radii,
    )
    update = (plane - scale[0, 0] * gradient.astype(F32)).astype(BF16)
    return update.reshape(1, 1, ROWS, N), loss.reshape(())


def solution(mesh):
    placed = (
        P("tile", "mask", "pencil", None),
        P("tile", "pencil", None),
        P(None, None, "pencil", None),
        P(),
        P("tile", None, "pencil"),
        P("tile", "pencil"),
    )
    return jax.shard_map(
        per_device,
        mesh=mesh,
        in_specs=placed,
        out_specs=(P("tile", "mask", "pencil", None), P()),
        check_vma=False,
    )
```

```python
import functools
import math

import jax
import jax.numpy as jnp
import numpy as np
from jax import lax
from jax.experimental import pallas as pl
from jax.experimental.pallas import tpu as pltpu
from jax.sharding import PartitionSpec as P
from ml_dtypes import bfloat16

N = 4096
KEEP = 256
HALF = 128
KERN = 4
ROWS = 128
SAMPLES = 512
PENCIL = 32
CHUNK = 512
PTS = 256
FIRST = 2
EPSILON = 1e-06
STEP_SIZE = 0.2
F32 = jnp.float32
BF16 = jnp.bfloat16
MESH = pl.DeviceIdType.MESH
VMEM = pltpu.VMEM
DMA = pltpu.SemaphoreType.DMA


def angles(first, second, period):
    return 2.0 * np.pi / period * ((first[:, None] * second[None, :]) % period)


@functools.cache
def tables():
    pixels = np.arange(N)
    freqs = np.arange(KEEP) - HALF
    half = np.arange(136)
    theta = angles(half, pixels, N)
    theta_cos, theta_sin = (np.cos(theta), np.sin(theta))
    theta_cos[129:], theta_sin[129:] = (0.0, 0.0)
    ahead = np.stack([theta_cos.reshape(17, 8, N), -theta_sin.reshape(17, 8, N)], axis=1).reshape(272, N)
    theta = angles(pixels, freqs, N)
    ahead_x = np.concatenate([np.cos(theta), np.sin(theta)], axis=1)
    theta_cos, theta_sin = (np.cos(theta), np.sin(theta))
    back_x = np.concatenate(
        [
            np.concatenate([theta_cos, -theta_sin], axis=1).reshape(PENCIL, ROWS, 512),
            np.concatenate([theta_sin, theta_cos], axis=1).reshape(PENCIL, ROWS, 512),
        ],
        axis=1,
    )
    theta = angles(np.abs(freqs), np.arange(SAMPLES), SAMPLES)
    sign = np.where(freqs < 0, -1.0, 1.0)[:, None]
    back_y = np.concatenate(
        [
            np.concatenate([np.cos(theta), sign * np.sin(theta)], axis=1),
            np.concatenate([-np.sin(theta), sign * np.cos(theta)], axis=1),
        ],
        axis=0,
    )
    shift = np.arange(N)
    bell = np.ones(N)
    for freq in range(1, 256):
        bell += 2.0 * np.cos(2.0 * np.pi / N * ((freq * shift) % N))
    bell /= SAMPLES
    bell += np.cos(2.0 * np.pi / N * ((256 * shift) % N)) / SAMPLES
    spread = bell[(pixels[None, :] - 8 * np.arange(SAMPLES)[:, None]) % N]
    pick = np.zeros((512, 256))
    for row in range(KEEP):
        a = abs(row - HALF)
        if a < HALF:
            pick[row, 16 * (a // 8) + a % 8] = 1.0
            pick[KEEP + row, 16 * (a // 8) + 8 + a % 8] = 1.0
    flip = np.zeros((KEEP, KEEP))
    for lane in range(1, KEEP):
        flip[KEEP - lane, lane] = 1.0
    return {
        "ahead": ahead.astype(bfloat16),
        "ahead_x": ahead_x.astype(bfloat16),
        "back_x": back_x.astype(bfloat16),
        "back_y": back_y.astype(bfloat16),
        "spread": spread.astype(bfloat16),
        "spread_t": np.ascontiguousarray(spread.T).astype(bfloat16),
        "pick": pick.astype(bfloat16),
        "merge": np.ascontiguousarray(pick.T).astype(bfloat16),
        "flip": flip.astype(bfloat16),
    }


def dot_nn(left, right):
    return lax.dot_general(left, right, (((1,), (0,)), ((), ())), preferred_element_type=F32)


def dot_nt(left, right):
    return lax.dot_general(left, right, (((1,), (1,)), ((), ())), preferred_element_type=F32)


def iota(shape, axis):
    return lax.broadcasted_iota(jnp.int32, shape, axis)


def each(low, high, body):
    def step(i, carry):
        body(i)
        return carry

    lax.fori_loop(low, high, step, 0)


def place():
    tile = lax.axis_index("tile")
    mask = lax.axis_index("mask")
    pencil = lax.axis_index("pencil")
    return tile, mask, pencil, pencil // 8, pencil % 8


def remote(src, dst, send, recv, where):
    return pltpu.make_async_remote_copy(
        src_ref=src, dst_ref=dst, send_sem=send, recv_sem=recv, device_id=where, device_id_type=MESH
    )


def step_kernel(
    mask_hbm, ahead_hbm, ahead_x_hbm, back_x_hbm, back_y_hbm, spread_hbm, target_hbm, spread_t_hbm,
    pick_ref, merge_ref, flip_ref, spectra_ref, points_ref, weights_ref, radii_ref,
    gradient_hbm, scale_out, loss_out,
    mask_ref, ahead_ref, ahead_x_ref, back_x, back_y, spread, target, spread_t,
    line_ref, lines_ref, seen, kern, slices, bands, fields, gap_ref, slope_ref, hot_ref, hot_t_ref,
    part_ref, gathered, summed, pieces, whole, note, notes, rounds, totals,
    load_sem, self_sem, kz_send, kz_recv, ka_send, ka_recv, kb_send, kb_recv, kd_send, kd_recv, ke_send, ke_recv, kc_send, kc_recv,
    a_send, a_recv, sz_send, sz_recv, sy_send, sy_recv,
    cy_send, cy_recv, cz_send, cz_recv, dz_send, dz_recv, dy_send, dy_recv, e_send, e_recv, f_send, f_recv, g_send, g_recv,
):
    tile, mask, pencil, y, z = place()
    chip, core = (tile // 2, tile % 2)
    owner = (z >= FIRST) & (z < FIRST + 4)
    column = z - FIRST
    load_mask = pltpu.make_async_copy(mask_hbm, mask_ref, load_sem.at[0])
    load_ahead = pltpu.make_async_copy(ahead_hbm, ahead_ref, load_sem.at[1])
    load_mask.start()
    load_ahead.start()
    barrier = pltpu.get_barrier_semaphore()

    def greet(where):
        pl.semaphore_signal(barrier, inc=1, device_id=where, device_id_type=MESH)

    each(1, 32, lambda d: greet({"pencil": (pencil + d) % 32}))
    each(0, 8, lambda d: greet({"mask": 1 - mask, "pencil": y * 8 + d}))
    each(1, 8, lambda d: greet({"tile": (tile + d) % 8}))

    sub = iota((8, KEEP), 0)
    lane = iota((8, KEEP), 1)
    freq_u = lane - HALF
    freq_v = sub + pencil * 8 - HALF
    radius = freq_u * freq_u + freq_v * freq_v
    parts = []
    for c in range(2):
        for k in range(KERN):
            limit = radii_ref[k] * radii_ref[k]
            parts.append(jnp.where(radius <= limit, spectra_ref[c, k], 0.0))
    plain = jnp.concatenate(parts, axis=0)
    turned = dot_nn(plain.astype(BF16), flip_ref[...])
    sign = jnp.where(iota((64, KEEP), 0) < 32, 1.0, -1.0)
    low = jnp.where(pencil < 16, 1.0, 0.0).astype(F32)
    plain = low * (turned * sign) + (1.0 - low) * plain
    spare = (sub == 1) & (lane == 0) & (pencil == 16)
    for part in range(8):
        rows = plain[part * 8 : part * 8 + 8]
        rest = rows - rows.astype(BF16).astype(F32)
        rows = jnp.where(spare, rest[0:1, HALF : HALF + 1], rows)
        slices[part] = jnp.concatenate([rows[:, :HALF], rows[:, HALF:]], axis=0).astype(BF16)
    kern[core, chip, y, z] = slices[tile]

    point_rows = points_ref[0].astype(F32) - (pencil * ROWS).astype(F32)
    point_cols = points_ref[1].astype(F32)
    normal = points_ref[2]
    step_row = jnp.where(normal == 0, 1.0, 0.0) - jnp.where(normal == 1, 1.0, 0.0)
    step_col = jnp.where(normal == 2, 1.0, 0.0) - jnp.where(normal == 3, 1.0, 0.0)
    flat = jnp.concatenate(
        [
            point_rows, point_rows - step_row, point_rows + step_row,
            point_cols, point_cols - step_col, point_cols + step_col,
            weights_ref[...], jnp.zeros((1, PTS), F32),
        ],
        axis=0,
    )
    tall = flat.T
    cols = jnp.concatenate([tall[:, 3:4], tall[:, 4:5], tall[:, 5:6]], axis=0).astype(jnp.int32)
    wide_rows = jnp.concatenate([flat[0:1], flat[1:2], flat[2:3]], axis=1).astype(jnp.int32)
    wide_cols = jnp.concatenate([flat[3:4], flat[4:5], flat[5:6]], axis=1).astype(jnp.int32)
    weight = jnp.concatenate([weights_ref[...]] * 3, axis=1)
    third = iota((1, 3 * PTS), 1)
    goal = jnp.where(third < PTS, 0.5, jnp.where(third < 2 * PTS, 1.0, 0.0))
    row_hot = jnp.where(iota((ROWS, 3 * PTS), 0) == wide_rows, 1.0, 0.0)

    load_mask.wait()
    load_ahead.wait()
    later = [
        pltpu.make_async_copy(ahead_x_hbm, ahead_x_ref, load_sem.at[2]),
        pltpu.make_async_copy(back_x_hbm.at[pencil], back_x, load_sem.at[3]),
        pltpu.make_async_copy(back_y_hbm, back_y, load_sem.at[4]),
        pltpu.make_async_copy(spread_hbm, spread, load_sem.at[5]),
        pltpu.make_async_copy(target_hbm, target, load_sem.at[6]),
        pltpu.make_async_copy(spread_t_hbm, spread_t, load_sem.at[7]),
    ]
    for load in later:
        load.start()
    line = dot_nt(ahead_ref[...], mask_ref[...].astype(BF16))
    lane8 = iota((8, ROWS), 1)
    cosine, sine = (line[256:264], line[264:272])
    both = jnp.where(lane8 < 64, cosine + pltpu.roll(cosine, 64, 1), sine + pltpu.roll(sine, 64, 1))
    empty = jnp.where(iota((8, ROWS), 0) == 0, both, line[8:16])
    line_ref[...] = jnp.concatenate([line[:8], empty, line[16:256]], axis=0).astype(BF16)

    pl.semaphore_wait(barrier, 46)

    def hop(rows, send, recv, other, spot, where):
        return remote(rows, rows, send.at[other], recv.at[spot], where)

    def kz(d, theirs=False):
        other = (z + d) % 8
        spot = other if theirs else z
        return hop(kern.at[core, chip, y, spot], kz_send, kz_recv, other, spot, {"pencil": y * 8 + other})

    def along_x(d, theirs):
        other = (chip + d) % 4
        return other, other if theirs else chip, {"tile": other * 2 + core}

    def along_y(d, theirs):
        other = (y + d) % 4
        return other, other if theirs else y, {"pencil": other * 8 + z}

    def ka(d, theirs=False):
        other, spot, where = along_x(d, theirs)
        return hop(kern.at[core, spot, y, pl.ds(0, 4)], ka_send, ka_recv, other, spot, where)

    def kb(d, theirs=False):
        other, spot, where = along_y(d, theirs)
        return hop(kern.at[core, chip, spot, pl.ds(4, 4)], kb_send, kb_recv, other, spot, where)

    def kd(d, theirs=False):
        other, spot, where = along_y(d, theirs)
        return hop(kern.at[core, pl.ds(0, 4), spot, pl.ds(0, 4)], kd_send, kd_recv, other, spot, where)

    def ke(d, theirs=False):
        other, spot, where = along_x(d, theirs)
        return hop(kern.at[core, spot, pl.ds(0, 4), pl.ds(4, 4)], ke_send, ke_recv, other, spot, where)

    def kc(half, theirs=False):
        side = 1 - core if theirs else core
        rows = kern.at[side, pl.ds(0, 4), pl.ds(0, 4), pl.ds(4 * half, 4)]
        return remote(rows, rows, kc_send.at[half], kc_recv.at[half], {"tile": chip * 2 + 1 - core})

    each(1, 8, lambda d: kz(d).start())

    own_lines = lines_ref.at[:, pl.ds(pl.multiple_of(pencil * ROWS, ROWS), ROWS)]

    def line_to(d):
        q = (pencil // 2 + d) % 16
        home = q // 4 * 8 + FIRST + q % 4
        src = line_ref.at[pl.ds(pl.multiple_of(q * 16, 16), 16)]
        return home, remote(src, own_lines, a_send.at[q], a_recv.at[pencil], {"pencil": home})

    def send_line(d):
        home, copy = line_to(d)

        @pl.when(home != pencil)
        def _():
            copy.start()

    each(0, 16, send_line)

    @pl.when(owner)
    def _():
        src = line_ref.at[pl.ds(pl.multiple_of((y * 4 + column) * 16, 16), 16)]
        keep = pltpu.make_async_copy(src, own_lines, self_sem)
        keep.start()
        keep.wait()

    each(1, 8, lambda d: kz(d, True).wait_recv())
    each(1, 4, lambda d: ka(d).start())
    each(1, 4, lambda d: kb(d).start())

    down = wide_cols - iota((128, 3 * PTS), 0)
    for base in range(0, N, 128):
        hot_t_ref[base : base + 128, :] = jnp.where(down == base, 1.0, 0.0).astype(BF16)

    each(1, 4, lambda d: ka(d, True).wait_recv())
    each(1, 4, lambda d: kd(d).start())
    each(1, 4, lambda d: kb(d, True).wait_recv())
    each(1, 4, lambda d: ke(d).start())

    def sz(d):
        spot = (mask * 8 + z + d) % 16
        mine = seen.at[y, mask, column]
        where = {"mask": spot // 8, "pencil": y * 8 + spot % 8}
        return remote(mine, mine, sz_send.at[spot], sz_recv.at[mask * 4 + column], where)

    later[0].wait()

    @pl.when(owner)
    def _():
        def line_from(d):
            other = (pencil + d) % 32
            src = line_ref.at[pl.ds(0, 16)]
            dst = lines_ref.at[:, pl.ds(pl.multiple_of(other * ROWS, ROWS), ROWS)]
            return remote(src, dst, a_send.at[0], a_recv.at[other], {"pencil": other})

        each(1, 32, lambda d: line_from(d).wait_recv())
        held = lines_ref[...].astype(F32)
        first = (y == 0) & (column == 0)
        stash = (iota((16, N), 0) == 8) & first
        extra = jnp.where(stash, held, 0.0)
        left = (iota((16, N), 1) % 128) < 64
        cos_sum = jnp.sum(jnp.where(left, extra, 0.0))
        sin_sum = jnp.sum(jnp.where(left, 0.0, extra))
        out = dot_nn(jnp.where(stash, 0.0, held).astype(BF16), ahead_x_ref[...])
        real = out[:8, :KEEP] + out[8:, KEEP:]
        imag = out[8:, :KEEP] - out[:8, KEEP:]
        slot = (sub == 0) & (lane == HALF + 1) & first
        real = jnp.where(slot, cos_sum, real)
        imag = jnp.where(slot, sin_sum, imag)
        still = (sub == 0) & (lane == HALF) & first
        imag = jnp.where(still, real - real.astype(BF16).astype(F32), imag)
        piece = jnp.concatenate([real, imag], axis=0) * (1.0 / (N * N))
        seen[y, mask, column] = piece.astype(BF16)
        each(1, 16, lambda d: sz(d).start())

    across = jnp.broadcast_to(cols, (3 * PTS, 128)) - iota((3 * PTS, 128), 1)
    for base in range(0, N, 128):
        hot_ref[:, base : base + 128] = jnp.where(across == base, 1.0, 0.0).astype(BF16)

    each(1, 4, lambda d: kd(d, True).wait_recv())
    kc(0).start()
    each(1, 4, lambda d: ke(d, True).wait_recv())
    kc(1).start()

    def sz_wait(m, q):
        theirs = seen.at[y, m, q]
        mine = (m == mask) & (q == column)

        @pl.when(jnp.logical_not(mine))
        def _():
            where = {"pencil": y * 8 + (z + 1) % 8}
            remote(theirs, theirs, sz_send.at[q], sz_recv.at[m * 4 + q], where).wait_recv()

    def sy(d, m, theirs=False):
        other = (y + d) % 4
        spot = other if theirs else y
        rows = seen.at[spot, m]
        return remote(rows, rows, sy_send.at[m, other], sy_recv.at[m, spot], {"pencil": other * 8 + z})

    def forward(m):
        each(0, 4, lambda q: sz_wait(m, q))
        each(1, 4, lambda d: sy(d, m).start())

    forward(mask)
    forward(1 - mask)
    kc(0, True).wait_recv()
    kc(1, True).wait_recv()

    slot = (sub == 0) & (lane == HALF + 1)
    still = (sub == 0) & (lane == HALF)

    for part in range(8):
        lines = kern[part % 2, part // 2].astype(F32).reshape(PENCIL, 16, HALF)
        bands[part] = jnp.concatenate(
            [lines[:, :8].reshape(KEEP, HALF), lines[:, 8:].reshape(KEEP, HALF)], axis=1
        )
        middle = bands[part, HALF : HALF + 8]
        rest = middle[1:2, 0:1]
        middle = jnp.where(still, middle + rest, jnp.where((sub == 1) & (lane == 0), 0.0, middle))
        bands[part, HALF : HALF + 8] = middle

    def spectrum(which):
        held = jnp.concatenate([seen[i, which].reshape(64, KEEP) for i in range(4)], axis=0)
        full = dot_nn(pick_ref[...], held)
        real, imag = (full[:KEEP], full[KEEP:])
        mid_real, mid_imag = (real[HALF : HALF + 8], imag[HALF : HALF + 8])
        edge_real = jnp.sum(jnp.where(slot, mid_real, 0.0))
        edge_imag = jnp.sum(jnp.where(slot, mid_imag, 0.0))
        mid_real = jnp.where(slot, pltpu.roll(mid_real, 2, 1), mid_real)
        mid_imag = jnp.where(slot, -pltpu.roll(mid_imag, 2, 1), mid_imag)
        mid_real = jnp.where(still, mid_real + mid_imag, mid_real)
        mid_imag = jnp.where(still, 0.0, mid_imag)
        top_real = jnp.where(sub == 0, edge_real, real[:8])
        top_imag = jnp.where(sub == 0, edge_imag, imag[:8])
        real = jnp.concatenate([top_real, real[8:HALF], mid_real, real[HALF + 8 :]], axis=0)
        imag = jnp.concatenate([top_imag, imag[8:HALF], mid_imag, imag[HALF + 8 :]], axis=0)
        return real, imag

    def remainder(band):
        middle = band[HALF : HALF + 8]
        return (middle - middle.astype(BF16).astype(F32))[0:1, HALF : HALF + 1]

    for load in later[1:]:
        load.wait()
    images = []
    for turn in range(2):
        which = mask if turn == 0 else 1 - mask
        each(1, 4, lambda d, which=which: sy(d, which, True).wait_recv())
        real, imag = spectrum(which)
        columned, rests, rests_imag = ([], [], [])
        for k in range(KERN):
            kern_real, kern_imag = (bands[k], bands[KERN + k])
            band_real = kern_real * real - kern_imag * imag
            band_imag = kern_real * imag + kern_imag * real
            band = jnp.concatenate([band_real, band_imag], axis=1).astype(BF16)
            out = dot_nt(back_x[...], band)
            out = jnp.concatenate([out[:ROWS], out[ROWS:]], axis=1)
            rounded = out.astype(BF16)
            columned.append(rounded)
            rest = out - rounded.astype(F32)
            rests.append(rest[:, HALF : HALF + 1] + remainder(band_real))
            rests_imag.append(rest[:, KEEP + HALF : KEEP + HALF + 1] + remainder(band_imag))
        field = dot_nn(jnp.concatenate(columned, axis=0), back_y[...])
        rest_real = jnp.broadcast_to(jnp.concatenate(rests, axis=0), (512, SAMPLES))
        rest_imag = jnp.broadcast_to(jnp.concatenate(rests_imag, axis=0), (512, SAMPLES))
        field = field + jnp.concatenate([rest_real, rest_imag], axis=1)
        if turn == 0:
            fields[...] = field.astype(BF16)
        square = field * field
        square = square[:, :SAMPLES] + square[:, SAMPLES:]
        images.append(square[:128] + square[128:256] + square[256:384] + square[384:])
    image = jnp.concatenate(images, axis=0).astype(BF16)

    loss = jnp.zeros((ROWS, 128), F32)
    picked = jnp.zeros((2 * ROWS, 3 * PTS), F32)
    for base in range(0, N, CHUNK):
        at = slice(base, base + CHUNK)
        fine = dot_nn(image, spread[:, at])
        clear = 0.5 - 0.5 * jnp.tanh(3.0 * fine - 1.5)
        own, other = (clear[:ROWS], clear[ROWS:])
        product = own * other
        union = 1.0 - product
        slope_ref[:, at] = 12.0 * product * (1.0 - own)
        gap = union - target[:, at].astype(F32)
        gap_ref[:, at] = gap
        high = union.astype(BF16)
        rest = (union - high.astype(F32)).astype(BF16)
        picked = picked + dot_nn(jnp.concatenate([high, rest], axis=0), hot_t_ref[at, :])
        square = gap * gap
        loss = loss + (square[:, :128] + square[:, 128:256]) + (square[:, 256:384] + square[:, 384:])
    missed = jnp.sum((picked[:ROWS] + picked[ROWS:]) * row_hot, axis=0, keepdims=True) - goal
    push = weight * missed
    loss = jnp.sum(loss) + jnp.sum(push * missed)
    hits = (row_hot * push).astype(BF16)
    drive = jnp.zeros((ROWS, SAMPLES), F32)
    for base in range(0, N, CHUNK):
        at = slice(base, base + CHUNK)
        pull = gap_ref[:, at] + dot_nn(hits, hot_ref[:, at])
        drive = drive + dot_nn((pull * slope_ref[:, at]).astype(BF16), spread_t[at, :])
    drive = jnp.concatenate([drive, drive], axis=1)
    drive = jnp.concatenate([drive] * KERN, axis=0)
    mixed = (drive * fields[...].astype(F32)).astype(BF16)
    lines = dot_nt(back_y[...], mixed)
    sum_real = jnp.zeros((KEEP, KEEP), F32)
    sum_imag = jnp.zeros((KEEP, KEEP), F32)
    for k in range(KERN):
        at = slice(k * ROWS, (k + 1) * ROWS)
        line = jnp.concatenate([lines[:KEEP, at], lines[KEEP:, at]], axis=1).astype(BF16)
        back = dot_nn(line, back_x[...])
        back_real, back_imag = (back[:, :KEEP], back[:, KEEP:])
        kern_real, kern_imag = (bands[k], bands[KERN + k])
        sum_real = sum_real + (kern_real * back_real + kern_imag * back_imag)
        sum_imag = sum_imag + (kern_real * back_imag - kern_imag * back_real)
    sum_real = sum_real * (2.0 / (N * N))
    sum_imag = sum_imag * (2.0 / (N * N))

    mid_real, mid_imag = (sum_real[HALF : HALF + 8], sum_imag[HALF : HALF + 8])
    turned = dot_nn(jnp.concatenate([mid_real, mid_imag], axis=0).astype(BF16), flip_ref[...])
    edge_real = jnp.sum(jnp.where(still, sum_real[:8], 0.0))
    edge_imag = jnp.sum(jnp.where(still, sum_imag[:8], 0.0))
    fold_real = jnp.where(lane < HALF, mid_real + turned[:8], jnp.where(lane == HALF, mid_real, 0.0))
    fold_imag = jnp.where(lane < HALF, mid_imag - turned[8:], 0.0)
    fold_real = jnp.where(lane == HALF + 1, edge_real, jnp.where(lane == HALF + 2, loss, fold_real))
    fold_imag = jnp.where(lane == HALF + 1, edge_imag, fold_imag)
    mid_real = jnp.where(sub == 0, fold_real, mid_real)
    mid_imag = jnp.where(sub == 0, fold_imag, mid_imag)
    full = jnp.concatenate(
        [
            sum_real[:HALF], mid_real, sum_real[HALF + 8 :],
            sum_imag[:HALF], mid_imag, sum_imag[HALF + 8 :],
        ],
        axis=0,
    ).astype(BF16)
    part_ref[...] = dot_nn(merge_ref[...], full).astype(BF16).reshape(4, 4, 16, KEEP)

    def cy(d, theirs=False):
        other = (y + d) % 4
        spot = other if theirs else y
        where = {"pencil": other * 8 + z}
        return remote(part_ref.at[other], gathered.at[spot], cy_send.at[other], cy_recv.at[spot], where)

    each(1, 4, lambda d: cy(d).start())
    gathered[y] = part_ref[y]
    each(1, 4, lambda d: cy(d, True).wait_recv())
    total = gathered[0].astype(F32) + gathered[1].astype(F32)
    total = total + (gathered[2].astype(F32) + gathered[3].astype(F32))
    summed[...] = total.astype(BF16)

    def cz(q):
        home = FIRST + q
        return home, remote(summed.at[q], pieces.at[z], cz_send.at[q], cz_recv.at[z], {"pencil": y * 8 + home})

    def send_piece(q):
        home, copy = cz(q)

        @pl.when(home != z)
        def _():
            copy.start()

    each(0, 4, send_piece)

    def dz(d):
        other = (z + d) % 8
        mine = whole.at[y, column]
        return remote(mine, mine, dz_send.at[other], dz_recv.at[column], {"pencil": y * 8 + other})

    row = iota((16, KEEP), 0)
    lane = iota((16, KEEP), 1)
    note_row = iota((8, 128), 0)

    def tell(d, theirs=False):
        other = (tile + d) % 8
        spot = other if theirs else tile
        return remote(note, notes.at[spot], e_send.at[other], e_recv.at[spot], {"tile": other})

    @pl.when(owner)
    def _():
        pieces[z] = summed[column]

        def piece_from(d):
            other = (z + d) % 8
            where = {"pencil": y * 8 + other}
            return remote(summed.at[0], pieces.at[other], cz_send.at[0], cz_recv.at[other], where)

        each(1, 8, lambda d: piece_from(d).wait_recv())
        one = pieces[...].astype(F32)
        one = (one[0] + one[1]) + (one[2] + one[3]) + (one[4] + one[5]) + (one[6] + one[7])
        whole[y, column] = one.astype(BF16)
        first = (y == 0) & (column == 0)
        loss = jnp.sum(jnp.where(first & (row == 0) & (lane == HALF + 2), one, 0.0))
        stash = first & ((row == 0) | (row == 8)) & (lane > HALF + 1)
        center = first & (row == 0) & (lane == HALF)
        energy = jnp.where(stash, 0.0, one * one) * jnp.where(center, 1.0, 0.5)
        energy = jnp.sum(energy)
        note[...] = jnp.where(note_row == 0, energy, jnp.where(note_row == 1, loss, 0.0))
        each(1, 8, lambda d: tell(d).start())
        notes[tile] = note[...]
        each(1, 8, lambda d: dz(d).start())

    def dz_wait(q):
        theirs = whole.at[y, q]

        @pl.when(q != column)
        def _():
            where = {"pencil": y * 8 + (z + 1) % 8}
            remote(theirs, theirs, dz_send.at[q], dz_recv.at[q], where).wait_recv()

    def dy(d, theirs=False):
        other = (y + d) % 4
        spot = other if theirs else y
        rows = whole.at[spot]
        return remote(rows, rows, dy_send.at[other], dy_recv.at[spot], {"pencil": other * 8 + z})

    def share(d):
        spot = (mask * 8 + z + d) % 16
        mine = rounds.at[mask * 4 + column]
        where = {"mask": spot // 8, "pencil": y * 8 + spot % 8}
        return remote(mine, mine, f_send.at[spot], f_recv.at[mask * 4 + column], where)

    @pl.when(owner)
    def _():
        each(1, 8, lambda d: tell(d, True).wait_recv())
        rounds[mask * 4 + column] = jnp.sum(notes[...], axis=0)
        each(1, 16, lambda d: share(d).start())

    each(0, 4, dz_wait)
    each(1, 4, lambda d: dy(d).start())

    def share_wait(s):
        theirs = rounds.at[s]

        @pl.when(jnp.logical_not((s // 4 == mask) & (s % 4 == column)))
        def _():
            where = {"pencil": y * 8 + (z + 1) % 8}
            remote(theirs, theirs, f_send.at[s], f_recv.at[s], where).wait_recv()

    each(0, 8, share_wait)
    totals[y] = jnp.sum(rounds[...], axis=0)

    def fy(d, theirs=False):
        other = (y + d) % 4
        spot = other if theirs else y
        rows = totals.at[spot]
        return remote(rows, rows, g_send.at[other], g_recv.at[spot], {"pencil": other * 8 + z})

    each(1, 4, lambda d: fy(d).start())

    each(1, 4, lambda d: dy(d, True).wait_recv())

    band = whole[...].astype(F32).reshape(KEEP, KEEP)
    head = band[:16]
    edge_real = jnp.sum(jnp.where((row == 0) & (lane == HALF + 1), head, 0.0))
    edge_imag = jnp.sum(jnp.where((row == 8) & (lane == HALF + 1), head, 0.0))
    head = jnp.where(((row == 0) | (row == 8)) & (lane > HALF), 0.0, head)
    band = jnp.concatenate([head, band[16:]], axis=0)
    pairs = band.reshape(16, 2, 8, KEEP)
    turned = jnp.concatenate([pairs[:, 1:2], -pairs[:, 0:1]], axis=1).reshape(KEEP, KEEP)
    stacked = jnp.concatenate([band, turned], axis=1).astype(BF16)
    lines = dot_nt(back_x[0:ROWS], stacked).astype(BF16)
    for base in range(0, N, CHUNK):
        at = slice(base, base + CHUNK)
        extra = ahead_ref[256:272, at].astype(F32)
        extra = edge_real * extra[0:1] + edge_imag * extra[8:9]
        target[:, at] = (dot_nn(lines, ahead_ref[0:256, at]) + extra).astype(BF16)
    store = pltpu.make_async_copy(target, gradient_hbm, load_sem.at[0])
    store.start()

    each(1, 8, lambda d: kz(d).wait_send())
    for step in (ka, kb, kd, ke):
        each(1, 4, lambda d, step=step: step(d).wait_send())
    kc(0).wait_send()
    kc(1).wait_send()
    each(1, 4, lambda d: sy(d, 0).wait_send())
    each(1, 4, lambda d: sy(d, 1).wait_send())
    each(1, 4, lambda d: cy(d).wait_send())
    each(1, 4, lambda d: dy(d).wait_send())

    def sent_line(d):
        home, copy = line_to(d)

        @pl.when(home != pencil)
        def _():
            copy.wait_send()

    each(0, 16, sent_line)

    def sent_piece(q):
        home, copy = cz(q)

        @pl.when(home != z)
        def _():
            copy.wait_send()

    each(0, 4, sent_piece)

    @pl.when(owner)
    def _():
        each(1, 16, lambda d: sz(d).wait_send())
        each(1, 8, lambda d: dz(d).wait_send())

    each(1, 4, lambda d: fy(d, True).wait_recv())
    total = (totals[0] + totals[1]) + (totals[2] + totals[3])
    scale_out[...] = STEP_SIZE * lax.rsqrt(total[0:1] * (1.0 / 16.0) + EPSILON)
    loss_out[0, 0] = jnp.sum(jnp.where(note_row == 1, total, 0.0)) * (0.5 / (128.0 * 8.0 * N * N))
    store.wait()
    each(1, 4, lambda d: fy(d).wait_send())

    @pl.when(owner)
    def _():
        each(1, 8, lambda d: tell(d).wait_send())
        each(1, 16, lambda d: share(d).wait_send())


ANY_SPEC = pl.BlockSpec(memory_space=pl.ANY)
VMEM_SPEC = pl.BlockSpec(memory_space=VMEM)
SMEM_SPEC = pl.BlockSpec(memory_space=pltpu.SMEM)
LIMIT = 56 * 1024 * 1024


def per_device(mask_field, design_target, kernel_spectra, support_radii, edge_points, point_weights):
    table = {name: jnp.asarray(value) for name, value in tables().items()}
    plane = mask_field.reshape(ROWS, N)
    gradient, scale, loss = pl.pallas_call(
        step_kernel,
        out_shape=(
            jax.ShapeDtypeStruct((ROWS, N), BF16),
            jax.ShapeDtypeStruct((1, 128), F32),
            jax.ShapeDtypeStruct((1, 1), F32),
        ),
        in_specs=[ANY_SPEC] * 8 + [VMEM_SPEC] * 6 + [SMEM_SPEC],
        out_specs=(ANY_SPEC, VMEM_SPEC, SMEM_SPEC),
        scratch_shapes=[
            VMEM((ROWS, N), F32),
            VMEM((272, N), BF16),
            VMEM((N, 512), BF16),
            VMEM((256, 512), BF16),
            VMEM((512, 1024), BF16),
            VMEM((SAMPLES, N), BF16),
            VMEM((ROWS, N), BF16),
            VMEM((N, SAMPLES), BF16),
            VMEM((256, ROWS), BF16),
            VMEM((16, N), BF16),
            VMEM((4, 2, 4, 16, KEEP), BF16),
            VMEM((2, 4, 4, 8, 16, HALF), BF16),
            VMEM((8, 16, HALF), BF16),
            VMEM((8, KEEP, KEEP), F32),
            VMEM((512, 1024), BF16),
            VMEM((ROWS, N), F32),
            VMEM((ROWS, N), F32),
            VMEM((3 * PTS, N), BF16),
            VMEM((N, 3 * PTS), BF16),
            VMEM((4, 4, 16, KEEP), BF16),
            VMEM((4, 4, 16, KEEP), BF16),
            VMEM((4, 16, KEEP), BF16),
            VMEM((8, 16, KEEP), BF16),
            VMEM((4, 4, 16, KEEP), BF16),
            VMEM((8, 128), F32),
            VMEM((8, 8, 128), F32),
            VMEM((8, 8, 128), F32),
            VMEM((4, 8, 128), F32),
            DMA((8,)),
            DMA,
        ]
        + [DMA((8,))] * 2
        + [DMA((4,))] * 8
        + [DMA((2,))] * 2
        + [DMA((16,)), DMA((32,)), DMA((16,)), DMA((8,)), DMA((2, 4)), DMA((2, 4))]
        + [DMA((4,)), DMA((4,)), DMA((4,)), DMA((8,)), DMA((8,)), DMA((4,)), DMA((4,)), DMA((4,))]
        + [DMA((8,)), DMA((8,)), DMA((16,)), DMA((8,)), DMA((4,)), DMA((4,))],
        compiler_params=pltpu.CompilerParams(collective_id=0, has_side_effects=True, vmem_limit_bytes=LIMIT),
        name="step_kernel",
    )(
        plane, table["ahead"], table["ahead_x"], table["back_x"], table["back_y"], table["spread"],
        design_target.reshape(ROWS, N), table["spread_t"], table["pick"], table["merge"], table["flip"],
        kernel_spectra, edge_points.reshape(3, 1, PTS), point_weights, support_radii,
    )
    update = (plane - scale[0, 0] * gradient.astype(F32)).astype(BF16)
    return update.reshape(1, 1, ROWS, N), loss.reshape(())


def solution(mesh):
    placed = (
        P("tile", "mask", "pencil", None),
        P("tile", "pencil", None),
        P(None, None, "pencil", None),
        P(),
        P("tile", None, "pencil"),
        P("tile", "pencil"),
    )
    return jax.shard_map(
        per_device,
        mesh=mesh,
        in_specs=placed,
        out_specs=(P("tile", "mask", "pencil", None), P()),
        check_vma=False,
    )
```

```python
import functools
import math

import jax
import jax.numpy as jnp
import numpy as np
from jax import lax
from jax.experimental import pallas as pl
from jax.experimental.pallas import tpu as pltpu
from jax.sharding import PartitionSpec as P
from ml_dtypes import bfloat16

N = 4096
KEEP = 256
HALF = 128
KERN = 4
ROWS = 128
SAMPLES = 512
PENCIL = 32
CHUNK = 512
PTS = 256
FIRST = 2
EPSILON = 1e-06
STEP_SIZE = 0.2
F32 = jnp.float32
BF16 = jnp.bfloat16
MESH = pl.DeviceIdType.MESH
VMEM = pltpu.VMEM
DMA = pltpu.SemaphoreType.DMA


def angles(first, second, period):
    return 2.0 * np.pi / period * ((first[:, None] * second[None, :]) % period)


@functools.cache
def tables():
    pixels = np.arange(N)
    freqs = np.arange(KEEP) - HALF
    half = np.arange(136)
    theta = angles(half, pixels, N)
    theta_cos, theta_sin = (np.cos(theta), np.sin(theta))
    theta_cos[129:], theta_sin[129:] = (0.0, 0.0)
    ahead = np.stack([theta_cos.reshape(17, 8, N), -theta_sin.reshape(17, 8, N)], axis=1).reshape(272, N)
    theta = angles(pixels, freqs, N)
    ahead_x = np.concatenate([np.cos(theta), np.sin(theta)], axis=1)
    theta_cos, theta_sin = (np.cos(theta), np.sin(theta))
    back_x = np.concatenate(
        [
            np.concatenate([theta_cos, -theta_sin], axis=1).reshape(PENCIL, ROWS, 512),
            np.concatenate([theta_sin, theta_cos], axis=1).reshape(PENCIL, ROWS, 512),
        ],
        axis=1,
    )
    theta = angles(np.abs(freqs), np.arange(SAMPLES), SAMPLES)
    sign = np.where(freqs < 0, -1.0, 1.0)[:, None]
    back_y = np.concatenate(
        [
            np.concatenate([np.cos(theta), sign * np.sin(theta)], axis=1),
            np.concatenate([-np.sin(theta), sign * np.cos(theta)], axis=1),
        ],
        axis=0,
    )
    shift = np.arange(N)
    bell = np.ones(N)
    for freq in range(1, 256):
        bell += 2.0 * np.cos(2.0 * np.pi / N * ((freq * shift) % N))
    bell /= SAMPLES
    bell += np.cos(2.0 * np.pi / N * ((256 * shift) % N)) / SAMPLES
    spread = bell[(pixels[None, :] - 8 * np.arange(SAMPLES)[:, None]) % N]
    pick = np.zeros((512, 256))
    for row in range(KEEP):
        a = abs(row - HALF)
        if a < HALF:
            pick[row, 16 * (a // 8) + a % 8] = 1.0
            pick[KEEP + row, 16 * (a // 8) + 8 + a % 8] = 1.0
    flip = np.zeros((KEEP, KEEP))
    for lane in range(1, KEEP):
        flip[KEEP - lane, lane] = 1.0
    return {
        "ahead": ahead.astype(bfloat16),
        "ahead_x": ahead_x.astype(bfloat16),
        "back_x": back_x.astype(bfloat16),
        "back_y": back_y.astype(bfloat16),
        "spread": spread.astype(bfloat16),
        "spread_t": np.ascontiguousarray(spread.T).astype(bfloat16),
        "pick": pick.astype(bfloat16),
        "merge": np.ascontiguousarray(pick.T).astype(bfloat16),
        "flip": flip.astype(bfloat16),
    }


def dot_nn(left, right):
    return lax.dot_general(left, right, (((1,), (0,)), ((), ())), preferred_element_type=F32)


def dot_nt(left, right):
    return lax.dot_general(left, right, (((1,), (1,)), ((), ())), preferred_element_type=F32)


def iota(shape, axis):
    return lax.broadcasted_iota(jnp.int32, shape, axis)


def each(low, high, body):
    for i in range(low, high):
        body(i)


def rem(value, by):
    return value % by if isinstance(value, int) else lax.rem(value, by)


def div(value, by):
    return value // by if isinstance(value, int) else lax.div(value, by)


def place():
    tile = lax.axis_index("tile")
    mask = lax.axis_index("mask")
    pencil = lax.axis_index("pencil")
    return tile, mask, pencil, div(pencil, 8), rem(pencil, 8)


def remote(src, dst, send, recv, where):
    return pltpu.make_async_remote_copy(
        src_ref=src, dst_ref=dst, send_sem=send, recv_sem=recv, device_id=where, device_id_type=MESH
    )


def step_kernel(
    mask_hbm, ahead_hbm, ahead_x_hbm, back_x_hbm, back_y_hbm, spread_hbm, target_hbm, spread_t_hbm,
    pick_ref, merge_ref, flip_ref, spectra_ref, points_ref, weights_ref, radii_ref,
    gradient_hbm, scale_out, loss_out,
    mask_ref, ahead_ref, ahead_x_ref, back_x, back_y, spread, target, spread_t,
    line_ref, lines_ref, seen, kern, slices, bands, fields, gap_ref, slope_ref, hot_ref, hot_t_ref,
    part_ref, gathered, summed, pieces, whole, note, notes, rounds, totals,
    load_sem, self_sem, kz_send, kz_recv, ka_send, ka_recv, kb_send, kb_recv, kd_send, kd_recv, ke_send, ke_recv, kc_send, kc_recv,
    a_send, a_recv, sz_send, sz_recv, sy_send, sy_recv,
    cy_send, cy_recv, cz_send, cz_recv, dz_send, dz_recv, dy_send, dy_recv, e_send, e_recv, f_send, f_recv, g_send, g_recv,
):
    tile, mask, pencil, y, z = place()
    chip, core = (div(tile, 2), rem(tile, 2))
    owner = (z >= FIRST) & (z < FIRST + 4)
    column = z - FIRST
    load_mask = pltpu.make_async_copy(mask_hbm, mask_ref, load_sem.at[0])
    load_ahead = pltpu.make_async_copy(ahead_hbm, ahead_ref, load_sem.at[1])
    load_mask.start()
    load_ahead.start()
    barrier = pltpu.get_barrier_semaphore()

    def greet(where):
        pl.semaphore_signal(barrier, inc=1, device_id=where, device_id_type=MESH)

    each(1, 32, lambda d: greet({"pencil": rem(pencil + d, 32)}))
    each(0, 8, lambda d: greet({"mask": 1 - mask, "pencil": y * 8 + d}))
    each(1, 8, lambda d: greet({"tile": rem(tile + d, 8)}))

    sub = iota((8, KEEP), 0)
    lane = iota((8, KEEP), 1)
    freq_u = lane - HALF
    freq_v = sub + pencil * 8 - HALF
    radius = freq_u * freq_u + freq_v * freq_v
    parts = []
    for c in range(2):
        for k in range(KERN):
            limit = radii_ref[k] * radii_ref[k]
            parts.append(jnp.where(radius <= limit, spectra_ref[c, k], 0.0))
    plain = jnp.concatenate(parts, axis=0)
    turned = dot_nn(plain.astype(BF16), flip_ref[...])
    sign = jnp.where(iota((64, KEEP), 0) < 32, 1.0, -1.0)
    low = jnp.where(pencil < 16, 1.0, 0.0).astype(F32)
    plain = low * (turned * sign) + (1.0 - low) * plain
    spare = (sub == 1) & (lane == 0) & (pencil == 16)
    for part in range(8):
        rows = plain[part * 8 : part * 8 + 8]
        rest = rows - rows.astype(BF16).astype(F32)
        rows = jnp.where(spare, rest[0:1, HALF : HALF + 1], rows)
        slices[part] = jnp.concatenate([rows[:, :HALF], rows[:, HALF:]], axis=0).astype(BF16)
    kern[core, chip, y, z] = slices[tile]

    point_rows = points_ref[0].astype(F32) - (pencil * ROWS).astype(F32)
    point_cols = points_ref[1].astype(F32)
    normal = points_ref[2]
    step_row = jnp.where(normal == 0, 1.0, 0.0) - jnp.where(normal == 1, 1.0, 0.0)
    step_col = jnp.where(normal == 2, 1.0, 0.0) - jnp.where(normal == 3, 1.0, 0.0)
    flat = jnp.concatenate(
        [
            point_rows, point_rows - step_row, point_rows + step_row,
            point_cols, point_cols - step_col, point_cols + step_col,
            weights_ref[...], jnp.zeros((1, PTS), F32),
        ],
        axis=0,
    )
    tall = flat.T
    cols = jnp.concatenate([tall[:, 3:4], tall[:, 4:5], tall[:, 5:6]], axis=0).astype(jnp.int32)
    wide_rows = jnp.concatenate([flat[0:1], flat[1:2], flat[2:3]], axis=1).astype(jnp.int32)
    wide_cols = jnp.concatenate([flat[3:4], flat[4:5], flat[5:6]], axis=1).astype(jnp.int32)
    weight = jnp.concatenate([weights_ref[...]] * 3, axis=1)
    third = iota((1, 3 * PTS), 1)
    goal = jnp.where(third < PTS, 0.5, jnp.where(third < 2 * PTS, 1.0, 0.0))
    row_hot = jnp.where(iota((ROWS, 3 * PTS), 0) == wide_rows, 1.0, 0.0)

    load_mask.wait()
    load_ahead.wait()
    later = [
        pltpu.make_async_copy(ahead_x_hbm, ahead_x_ref, load_sem.at[2]),
        pltpu.make_async_copy(back_x_hbm.at[pencil], back_x, load_sem.at[3]),
        pltpu.make_async_copy(back_y_hbm, back_y, load_sem.at[4]),
        pltpu.make_async_copy(spread_hbm, spread, load_sem.at[5]),
        pltpu.make_async_copy(target_hbm, target, load_sem.at[6]),
        pltpu.make_async_copy(spread_t_hbm, spread_t, load_sem.at[7]),
    ]
    for load in later:
        load.start()
    line = dot_nt(ahead_ref[...], mask_ref[...].astype(BF16))
    lane8 = iota((8, ROWS), 1)
    cosine, sine = (line[256:264], line[264:272])
    both = jnp.where(lane8 < 64, cosine + pltpu.roll(cosine, 64, 1), sine + pltpu.roll(sine, 64, 1))
    empty = jnp.where(iota((8, ROWS), 0) == 0, both, line[8:16])
    line_ref[...] = jnp.concatenate([line[:8], empty, line[16:256]], axis=0).astype(BF16)

    pl.semaphore_wait(barrier, 46)

    def hop(rows, send, recv, other, spot, where):
        return remote(rows, rows, send.at[other], recv.at[spot], where)

    def kz(d, theirs=False):
        other = rem(z + d, 8)
        spot = other if theirs else z
        return hop(kern.at[core, chip, y, spot], kz_send, kz_recv, other, spot, {"pencil": y * 8 + other})

    def along_x(d, theirs):
        other = rem(chip + d, 4)
        return other, other if theirs else chip, {"tile": other * 2 + core}

    def along_y(d, theirs):
        other = rem(y + d, 4)
        return other, other if theirs else y, {"pencil": other * 8 + z}

    def ka(d, theirs=False):
        other, spot, where = along_x(d, theirs)
        return hop(kern.at[core, spot, y, pl.ds(0, 4)], ka_send, ka_recv, other, spot, where)

    def kb(d, theirs=False):
        other, spot, where = along_y(d, theirs)
        return hop(kern.at[core, chip, spot, pl.ds(4, 4)], kb_send, kb_recv, other, spot, where)

    def kd(d, theirs=False):
        other, spot, where = along_y(d, theirs)
        return hop(kern.at[core, pl.ds(0, 4), spot, pl.ds(0, 4)], kd_send, kd_recv, other, spot, where)

    def ke(d, theirs=False):
        other, spot, where = along_x(d, theirs)
        return hop(kern.at[core, spot, pl.ds(0, 4), pl.ds(4, 4)], ke_send, ke_recv, other, spot, where)

    def kc(half, theirs=False):
        side = 1 - core if theirs else core
        rows = kern.at[side, pl.ds(0, 4), pl.ds(0, 4), pl.ds(4 * half, 4)]
        return remote(rows, rows, kc_send.at[half], kc_recv.at[half], {"tile": chip * 2 + 1 - core})

    each(1, 8, lambda d: kz(d).start())

    own_lines = lines_ref.at[:, pl.ds(pl.multiple_of(pencil * ROWS, ROWS), ROWS)]

    def line_to(d):
        q = rem(div(pencil, 2) + d, 16)
        home = div(q, 4) * 8 + FIRST + rem(q, 4)
        src = line_ref.at[pl.ds(pl.multiple_of(q * 16, 16), 16)]
        return home, remote(src, own_lines, a_send.at[q], a_recv, {"pencil": home})

    def send_line(d):
        home, copy = line_to(d)

        @pl.when(home != pencil)
        def _():
            copy.start()

    each(0, 16, send_line)

    @pl.when(owner)
    def _():
        src = line_ref.at[pl.ds(pl.multiple_of((y * 4 + column) * 16, 16), 16)]
        keep = pltpu.make_async_copy(src, own_lines, self_sem)
        keep.start()
        keep.wait()

    each(1, 8, lambda d: kz(d, True).wait_recv())
    each(1, 4, lambda d: ka(d).start())
    each(1, 4, lambda d: kb(d).start())

    down = wide_cols - iota((128, 3 * PTS), 0)
    for base in range(0, N, 128):
        hot_t_ref[base : base + 128, :] = jnp.where(down == base, 1.0, 0.0).astype(BF16)

    each(1, 4, lambda d: ka(d, True).wait_recv())
    each(1, 4, lambda d: kd(d).start())
    each(1, 4, lambda d: kb(d, True).wait_recv())
    each(1, 4, lambda d: ke(d).start())

    def sz(d):
        side = mask if d < 8 else 1 - mask
        other = rem(z + d, 8)
        mine = seen.at[y, mask, column]
        where = {"mask": side, "pencil": y * 8 + other}
        return remote(mine, mine, sz_send.at[side * 8 + other], sz_recv.at[mask * 4 + column], where)

    later[0].wait()

    @pl.when(owner)
    def _():
        others = lines_ref.at[:, pl.ds(0, 31 * ROWS)]
        remote(others, others, a_send.at[0], a_recv, {"pencil": rem(pencil + 1, 32)}).wait_recv()
        held = lines_ref[...].astype(F32)
        first = (y == 0) & (column == 0)
        stash = (iota((16, N), 0) == 8) & first
        extra = jnp.where(stash, held, 0.0)
        left = (iota((16, N), 1) % 128) < 64
        cos_sum = jnp.sum(jnp.where(left, extra, 0.0))
        sin_sum = jnp.sum(jnp.where(left, 0.0, extra))
        out = dot_nn(jnp.where(stash, 0.0, held).astype(BF16), ahead_x_ref[...])
        real = out[:8, :KEEP] + out[8:, KEEP:]
        imag = out[8:, :KEEP] - out[:8, KEEP:]
        slot = (sub == 0) & (lane == HALF + 1) & first
        real = jnp.where(slot, cos_sum, real)
        imag = jnp.where(slot, sin_sum, imag)
        still = (sub == 0) & (lane == HALF) & first
        imag = jnp.where(still, real - real.astype(BF16).astype(F32), imag)
        piece = jnp.concatenate([real, imag], axis=0) * (1.0 / (N * N))
        seen[y, mask, column] = piece.astype(BF16)
        each(1, 16, lambda d: sz(d).start())

    across = jnp.broadcast_to(cols, (3 * PTS, 128)) - iota((3 * PTS, 128), 1)
    for base in range(0, N, 128):
        hot_ref[:, base : base + 128] = jnp.where(across == base, 1.0, 0.0).astype(BF16)

    each(1, 4, lambda d: kd(d, True).wait_recv())
    kc(0).start()
    each(1, 4, lambda d: ke(d, True).wait_recv())
    kc(1).start()

    def sz_wait(m, q):
        theirs = seen.at[y, m, q]
        mine = (m == mask) & (q == column)

        @pl.when(jnp.logical_not(mine))
        def _():
            where = {"pencil": y * 8 + rem(z + 1, 8)}
            remote(theirs, theirs, sz_send.at[q], sz_recv.at[m * 4 + q], where).wait_recv()

    def sy(d, m, theirs=False):
        other = rem(y + d, 4)
        spot = other if theirs else y
        rows = seen.at[spot, m]
        return remote(rows, rows, sy_send.at[m, other], sy_recv.at[m, spot], {"pencil": other * 8 + z})

    def forward(m):
        each(0, 4, lambda q: sz_wait(m, q))
        each(1, 4, lambda d: sy(d, m).start())

    forward(mask)
    forward(1 - mask)
    kc(0, True).wait_recv()
    kc(1, True).wait_recv()

    slot = (sub == 0) & (lane == HALF + 1)
    still = (sub == 0) & (lane == HALF)

    for part in range(8):
        lines = kern[part % 2, part // 2].astype(F32).reshape(PENCIL, 16, HALF)
        bands[part] = jnp.concatenate(
            [lines[:, :8].reshape(KEEP, HALF), lines[:, 8:].reshape(KEEP, HALF)], axis=1
        )
        middle = bands[part, HALF : HALF + 8]
        rest = middle[1:2, 0:1]
        middle = jnp.where(still, middle + rest, jnp.where((sub == 1) & (lane == 0), 0.0, middle))
        bands[part, HALF : HALF + 8] = middle

    def spectrum(which):
        held = jnp.concatenate([seen[i, which].reshape(64, KEEP) for i in range(4)], axis=0)
        full = dot_nn(pick_ref[...], held)
        real, imag = (full[:KEEP], full[KEEP:])
        mid_real, mid_imag = (real[HALF : HALF + 8], imag[HALF : HALF + 8])
        edge_real = jnp.sum(jnp.where(slot, mid_real, 0.0))
        edge_imag = jnp.sum(jnp.where(slot, mid_imag, 0.0))
        mid_real = jnp.where(slot, pltpu.roll(mid_real, 2, 1), mid_real)
        mid_imag = jnp.where(slot, -pltpu.roll(mid_imag, 2, 1), mid_imag)
        mid_real = jnp.where(still, mid_real + mid_imag, mid_real)
        mid_imag = jnp.where(still, 0.0, mid_imag)
        top_real = jnp.where(sub == 0, edge_real, real[:8])
        top_imag = jnp.where(sub == 0, edge_imag, imag[:8])
        real = jnp.concatenate([top_real, real[8:HALF], mid_real, real[HALF + 8 :]], axis=0)
        imag = jnp.concatenate([top_imag, imag[8:HALF], mid_imag, imag[HALF + 8 :]], axis=0)
        return real, imag

    def remainder(band):
        middle = band[HALF : HALF + 8]
        return (middle - middle.astype(BF16).astype(F32))[0:1, HALF : HALF + 1]

    for load in later[1:]:
        load.wait()
    images = []
    for turn in range(2):
        which = mask if turn == 0 else 1 - mask
        each(1, 4, lambda d, which=which: sy(d, which, True).wait_recv())
        real, imag = spectrum(which)
        columned, rests, rests_imag = ([], [], [])
        for k in range(KERN):
            kern_real, kern_imag = (bands[k], bands[KERN + k])
            band_real = kern_real * real - kern_imag * imag
            band_imag = kern_real * imag + kern_imag * real
            band = jnp.concatenate([band_real, band_imag], axis=1).astype(BF16)
            out = dot_nt(back_x[...], band)
            out = jnp.concatenate([out[:ROWS], out[ROWS:]], axis=1)
            rounded = out.astype(BF16)
            columned.append(rounded)
            rest = out - rounded.astype(F32)
            rests.append(rest[:, HALF : HALF + 1] + remainder(band_real))
            rests_imag.append(rest[:, KEEP + HALF : KEEP + HALF + 1] + remainder(band_imag))
        field = dot_nn(jnp.concatenate(columned, axis=0), back_y[...])
        rest_real = jnp.broadcast_to(jnp.concatenate(rests, axis=0), (512, SAMPLES))
        rest_imag = jnp.broadcast_to(jnp.concatenate(rests_imag, axis=0), (512, SAMPLES))
        field = field + jnp.concatenate([rest_real, rest_imag], axis=1)
        if turn == 0:
            fields[...] = field.astype(BF16)
        square = field * field
        square = square[:, :SAMPLES] + square[:, SAMPLES:]
        images.append(square[:128] + square[128:256] + square[256:384] + square[384:])
    image = jnp.concatenate(images, axis=0).astype(BF16)

    loss = jnp.zeros((ROWS, 128), F32)
    picked = jnp.zeros((2 * ROWS, 3 * PTS), F32)
    for base in range(0, N, CHUNK):
        at = slice(base, base + CHUNK)
        fine = dot_nn(image, spread[:, at])
        clear = 0.5 - 0.5 * jnp.tanh(3.0 * fine - 1.5)
        own, other = (clear[:ROWS], clear[ROWS:])
        product = own * other
        union = 1.0 - product
        slope_ref[:, at] = 12.0 * product * (1.0 - own)
        gap = union - target[:, at].astype(F32)
        gap_ref[:, at] = gap
        high = union.astype(BF16)
        rest = (union - high.astype(F32)).astype(BF16)
        picked = picked + dot_nn(jnp.concatenate([high, rest], axis=0), hot_t_ref[at, :])
        square = gap * gap
        loss = loss + (square[:, :128] + square[:, 128:256]) + (square[:, 256:384] + square[:, 384:])
    missed = jnp.sum((picked[:ROWS] + picked[ROWS:]) * row_hot, axis=0, keepdims=True) - goal
    push = weight * missed
    loss = jnp.sum(loss) + jnp.sum(push * missed)
    hits = (row_hot * push).astype(BF16)
    drive = jnp.zeros((ROWS, SAMPLES), F32)
    for base in range(0, N, CHUNK):
        at = slice(base, base + CHUNK)
        pull = gap_ref[:, at] + dot_nn(hits, hot_ref[:, at])
        drive = drive + dot_nn((pull * slope_ref[:, at]).astype(BF16), spread_t[at, :])
    drive = jnp.concatenate([drive, drive], axis=1)
    drive = jnp.concatenate([drive] * KERN, axis=0)
    mixed = (drive * fields[...].astype(F32)).astype(BF16)
    lines = dot_nt(back_y[...], mixed)
    sum_real = jnp.zeros((KEEP, KEEP), F32)
    sum_imag = jnp.zeros((KEEP, KEEP), F32)
    for k in range(KERN):
        at = slice(k * ROWS, (k + 1) * ROWS)
        line = jnp.concatenate([lines[:KEEP, at], lines[KEEP:, at]], axis=1).astype(BF16)
        back = dot_nn(line, back_x[...])
        back_real, back_imag = (back[:, :KEEP], back[:, KEEP:])
        kern_real, kern_imag = (bands[k], bands[KERN + k])
        sum_real = sum_real + (kern_real * back_real + kern_imag * back_imag)
        sum_imag = sum_imag + (kern_real * back_imag - kern_imag * back_real)
    sum_real = sum_real * (2.0 / (N * N))
    sum_imag = sum_imag * (2.0 / (N * N))

    mid_real, mid_imag = (sum_real[HALF : HALF + 8], sum_imag[HALF : HALF + 8])
    turned = dot_nn(jnp.concatenate([mid_real, mid_imag], axis=0).astype(BF16), flip_ref[...])
    edge_real = jnp.sum(jnp.where(still, sum_real[:8], 0.0))
    edge_imag = jnp.sum(jnp.where(still, sum_imag[:8], 0.0))
    fold_real = jnp.where(lane < HALF, mid_real + turned[:8], jnp.where(lane == HALF, mid_real, 0.0))
    fold_imag = jnp.where(lane < HALF, mid_imag - turned[8:], 0.0)
    fold_real = jnp.where(lane == HALF + 1, edge_real, jnp.where(lane == HALF + 2, loss, fold_real))
    fold_imag = jnp.where(lane == HALF + 1, edge_imag, fold_imag)
    mid_real = jnp.where(sub == 0, fold_real, mid_real)
    mid_imag = jnp.where(sub == 0, fold_imag, mid_imag)
    full = jnp.concatenate(
        [
            sum_real[:HALF], mid_real, sum_real[HALF + 8 :],
            sum_imag[:HALF], mid_imag, sum_imag[HALF + 8 :],
        ],
        axis=0,
    ).astype(BF16)
    part_ref[...] = dot_nn(merge_ref[...], full).astype(BF16).reshape(4, 4, 16, KEEP)

    def cy(d, theirs=False):
        other = rem(y + d, 4)
        spot = other if theirs else y
        where = {"pencil": other * 8 + z}
        return remote(part_ref.at[other], gathered.at[spot], cy_send.at[other], cy_recv.at[spot], where)

    each(1, 4, lambda d: cy(d).start())
    gathered[y] = part_ref[y]
    each(1, 4, lambda d: cy(d, True).wait_recv())
    total = gathered[0].astype(F32) + gathered[1].astype(F32)
    total = total + (gathered[2].astype(F32) + gathered[3].astype(F32))
    summed[...] = total.astype(BF16)

    def cz(q):
        home = FIRST + q
        return home, remote(summed.at[q], pieces.at[z], cz_send.at[q], cz_recv.at[z], {"pencil": y * 8 + home})

    def send_piece(q):
        home, copy = cz(q)

        @pl.when(home != z)
        def _():
            copy.start()

    each(0, 4, send_piece)

    def dz(d):
        other = rem(z + d, 8)
        mine = whole.at[y, column]
        return remote(mine, mine, dz_send.at[other], dz_recv.at[column], {"pencil": y * 8 + other})

    row = iota((16, KEEP), 0)
    lane = iota((16, KEEP), 1)
    note_row = iota((8, 128), 0)

    def tell(d, theirs=False):
        other = rem(tile + d, 8)
        spot = other if theirs else tile
        return remote(note, notes.at[spot], e_send.at[other], e_recv.at[spot], {"tile": other})

    @pl.when(owner)
    def _():
        pieces[z] = summed[column]

        def piece_from(d):
            other = rem(z + d, 8)
            where = {"pencil": y * 8 + other}
            return remote(summed.at[0], pieces.at[other], cz_send.at[0], cz_recv.at[other], where)

        each(1, 8, lambda d: piece_from(d).wait_recv())
        one = pieces[...].astype(F32)
        one = (one[0] + one[1]) + (one[2] + one[3]) + (one[4] + one[5]) + (one[6] + one[7])
        whole[y, column] = one.astype(BF16)
        first = (y == 0) & (column == 0)
        loss = jnp.sum(jnp.where(first & (row == 0) & (lane == HALF + 2), one, 0.0))
        stash = first & ((row == 0) | (row == 8)) & (lane > HALF + 1)
        center = first & (row == 0) & (lane == HALF)
        energy = jnp.where(stash, 0.0, one * one) * jnp.where(center, 1.0, 0.5)
        energy = jnp.sum(energy)
        note[...] = jnp.where(note_row == 0, energy, jnp.where(note_row == 1, loss, 0.0))
        each(1, 8, lambda d: tell(d).start())
        notes[tile] = note[...]
        each(1, 8, lambda d: dz(d).start())

    def dz_wait(q):
        theirs = whole.at[y, q]

        @pl.when(q != column)
        def _():
            where = {"pencil": y * 8 + rem(z + 1, 8)}
            remote(theirs, theirs, dz_send.at[q], dz_recv.at[q], where).wait_recv()

    def dy(d, theirs=False):
        other = rem(y + d, 4)
        spot = other if theirs else y
        rows = whole.at[spot]
        return remote(rows, rows, dy_send.at[other], dy_recv.at[spot], {"pencil": other * 8 + z})

    def share(step):
        d = 8 + div(step, 2) * (1 if step % 2 else -1)
        spot = rem(mask * 8 + z + d, 16)
        mine = rounds.at[mask * 4 + column]
        where = {"mask": div(spot, 8), "pencil": y * 8 + rem(spot, 8)}
        return remote(mine, mine, f_send.at[spot], f_recv.at[mask * 4 + column], where)

    @pl.when(owner)
    def _():
        each(1, 8, lambda d: tell(d, True).wait_recv())
        rounds[mask * 4 + column] = jnp.sum(notes[...], axis=0)
        each(1, 16, lambda d: share(d).start())

    each(0, 4, dz_wait)
    each(1, 4, lambda d: dy(d).start())

    def share_wait(s):
        theirs = rounds.at[s]

        @pl.when(jnp.logical_not((s // 4 == mask) & (s % 4 == column)))
        def _():
            where = {"pencil": y * 8 + rem(z + 1, 8)}
            remote(theirs, theirs, f_send.at[s], f_recv.at[s], where).wait_recv()

    each(0, 8, share_wait)
    totals[y] = jnp.sum(rounds[...], axis=0)

    def fy(d, theirs=False):
        other = rem(y + d, 4)
        spot = other if theirs else y
        rows = totals.at[spot]
        return remote(rows, rows, g_send.at[other], g_recv.at[spot], {"pencil": other * 8 + z})

    each(1, 4, lambda d: fy(d).start())

    each(1, 4, lambda d: dy(d, True).wait_recv())

    band = whole[...].astype(F32).reshape(KEEP, KEEP)
    head = band[:16]
    edge_real = jnp.sum(jnp.where((row == 0) & (lane == HALF + 1), head, 0.0))
    edge_imag = jnp.sum(jnp.where((row == 8) & (lane == HALF + 1), head, 0.0))
    head = jnp.where(((row == 0) | (row == 8)) & (lane > HALF), 0.0, head)
    band = jnp.concatenate([head, band[16:]], axis=0)
    pairs = band.reshape(16, 2, 8, KEEP)
    turned = jnp.concatenate([pairs[:, 1:2], -pairs[:, 0:1]], axis=1).reshape(KEEP, KEEP)
    stacked = jnp.concatenate([band, turned], axis=1).astype(BF16)
    lines = dot_nt(back_x[0:ROWS], stacked).astype(BF16)
    for base in range(0, N, CHUNK):
        at = slice(base, base + CHUNK)
        extra = ahead_ref[256:272, at].astype(F32)
        extra = edge_real * extra[0:1] + edge_imag * extra[8:9]
        target[:, at] = (dot_nn(lines, ahead_ref[0:256, at]) + extra).astype(BF16)
    store = pltpu.make_async_copy(target, gradient_hbm, load_sem.at[0])
    store.start()

    each(1, 8, lambda d: kz(d).wait_send())
    for step in (ka, kb, kd, ke):
        each(1, 4, lambda d, step=step: step(d).wait_send())
    kc(0).wait_send()
    kc(1).wait_send()
    each(1, 4, lambda d: sy(d, 0).wait_send())
    each(1, 4, lambda d: sy(d, 1).wait_send())
    each(1, 4, lambda d: cy(d).wait_send())
    each(1, 4, lambda d: dy(d).wait_send())

    def sent_line(d):
        home, copy = line_to(d)

        @pl.when(home != pencil)
        def _():
            copy.wait_send()

    each(0, 16, sent_line)

    def sent_piece(q):
        home, copy = cz(q)

        @pl.when(home != z)
        def _():
            copy.wait_send()

    each(0, 4, sent_piece)

    @pl.when(owner)
    def _():
        each(1, 16, lambda d: sz(d).wait_send())
        each(1, 8, lambda d: dz(d).wait_send())

    each(1, 4, lambda d: fy(d, True).wait_recv())
    total = (totals[0] + totals[1]) + (totals[2] + totals[3])
    scale_out[...] = STEP_SIZE * lax.rsqrt(total[0:1] * (1.0 / 16.0) + EPSILON)
    loss_out[0, 0] = jnp.sum(jnp.where(note_row == 1, total, 0.0)) * (0.5 / (128.0 * 8.0 * N * N))
    store.wait()
    each(1, 4, lambda d: fy(d).wait_send())

    @pl.when(owner)
    def _():
        each(1, 8, lambda d: tell(d).wait_send())
        each(1, 16, lambda d: share(d).wait_send())


ANY_SPEC = pl.BlockSpec(memory_space=pl.ANY)
VMEM_SPEC = pl.BlockSpec(memory_space=VMEM)
SMEM_SPEC = pl.BlockSpec(memory_space=pltpu.SMEM)
LIMIT = 56 * 1024 * 1024


def per_device(mask_field, design_target, kernel_spectra, support_radii, edge_points, point_weights):
    table = {name: jnp.asarray(value) for name, value in tables().items()}
    plane = mask_field.reshape(ROWS, N)
    gradient, scale, loss = pl.pallas_call(
        step_kernel,
        out_shape=(
            jax.ShapeDtypeStruct((ROWS, N), BF16),
            jax.ShapeDtypeStruct((1, 128), F32),
            jax.ShapeDtypeStruct((1, 1), F32),
        ),
        in_specs=[ANY_SPEC] * 8 + [VMEM_SPEC] * 6 + [SMEM_SPEC],
        out_specs=(ANY_SPEC, VMEM_SPEC, SMEM_SPEC),
        scratch_shapes=[
            VMEM((ROWS, N), F32),
            VMEM((272, N), BF16),
            VMEM((N, 512), BF16),
            VMEM((256, 512), BF16),
            VMEM((512, 1024), BF16),
            VMEM((SAMPLES, N), BF16),
            VMEM((ROWS, N), BF16),
            VMEM((N, SAMPLES), BF16),
            VMEM((256, ROWS), BF16),
            VMEM((16, N), BF16),
            VMEM((4, 2, 4, 16, KEEP), BF16),
            VMEM((2, 4, 4, 8, 16, HALF), BF16),
            VMEM((8, 16, HALF), BF16),
            VMEM((8, KEEP, KEEP), F32),
            VMEM((512, 1024), BF16),
            VMEM((ROWS, N), F32),
            VMEM((ROWS, N), F32),
            VMEM((3 * PTS, N), BF16),
            VMEM((N, 3 * PTS), BF16),
            VMEM((4, 4, 16, KEEP), BF16),
            VMEM((4, 4, 16, KEEP), BF16),
            VMEM((4, 16, KEEP), BF16),
            VMEM((8, 16, KEEP), BF16),
            VMEM((4, 4, 16, KEEP), BF16),
            VMEM((8, 128), F32),
            VMEM((8, 8, 128), F32),
            VMEM((8, 8, 128), F32),
            VMEM((4, 8, 128), F32),
            DMA((8,)),
            DMA,
        ]
        + [DMA((8,))] * 2
        + [DMA((4,))] * 8
        + [DMA((2,))] * 2
        + [DMA((16,)), DMA, DMA((16,)), DMA((8,)), DMA((2, 4)), DMA((2, 4))]
        + [DMA((4,)), DMA((4,)), DMA((4,)), DMA((8,)), DMA((8,)), DMA((4,)), DMA((4,)), DMA((4,))]
        + [DMA((8,)), DMA((8,)), DMA((16,)), DMA((8,)), DMA((4,)), DMA((4,))],
        compiler_params=pltpu.CompilerParams(collective_id=0, has_side_effects=True, vmem_limit_bytes=LIMIT),
        name="step_kernel",
    )(
        plane, table["ahead"], table["ahead_x"], table["back_x"], table["back_y"], table["spread"],
        design_target.reshape(ROWS, N), table["spread_t"], table["pick"], table["merge"], table["flip"],
        kernel_spectra, edge_points.reshape(3, 1, PTS), point_weights, support_radii,
    )
    update = (plane - scale[0, 0] * gradient.astype(F32)).astype(BF16)
    return update.reshape(1, 1, ROWS, N), loss.reshape(())


def solution(mesh):
    placed = (
        P("tile", "mask", "pencil", None),
        P("tile", "pencil", None),
        P(None, None, "pencil", None),
        P(),
        P("tile", None, "pencil"),
        P("tile", "pencil"),
    )
    return jax.shard_map(
        per_device,
        mesh=mesh,
        in_specs=placed,
        out_specs=(P("tile", "mask", "pencil", None), P()),
        check_vma=False,
    )
```

```python
import functools
import math

import jax
import jax.numpy as jnp
import numpy as np
from jax import lax
from jax.experimental import pallas as pl
from jax.experimental.pallas import tpu as pltpu
from jax.sharding import PartitionSpec as P
from ml_dtypes import bfloat16

N = 4096
KEEP = 256
HALF = 128
KERN = 4
ROWS = 128
SAMPLES = 512
PENCIL = 32
CHUNK = 512
PTS = 256
FIRST = 2
EPSILON = 1e-06
STEP_SIZE = 0.2
F32 = jnp.float32
BF16 = jnp.bfloat16
MESH = pl.DeviceIdType.MESH
VMEM = pltpu.VMEM
DMA = pltpu.SemaphoreType.DMA


def angles(first, second, period):
    return 2.0 * np.pi / period * ((first[:, None] * second[None, :]) % period)


@functools.cache
def tables():
    pixels = np.arange(N)
    freqs = np.arange(KEEP) - HALF
    half = np.arange(136)
    theta = angles(half, pixels, N)
    theta_cos, theta_sin = (np.cos(theta), np.sin(theta))
    theta_cos[129:], theta_sin[129:] = (0.0, 0.0)
    ahead = np.stack([theta_cos.reshape(17, 8, N), -theta_sin.reshape(17, 8, N)], axis=1).reshape(272, N)
    theta = angles(pixels, freqs, N)
    ahead_x = np.concatenate([np.cos(theta), np.sin(theta)], axis=1)
    theta_cos, theta_sin = (np.cos(theta), np.sin(theta))
    back_x = np.concatenate(
        [
            np.concatenate([theta_cos, -theta_sin], axis=1).reshape(PENCIL, ROWS, 512),
            np.concatenate([theta_sin, theta_cos], axis=1).reshape(PENCIL, ROWS, 512),
        ],
        axis=1,
    )
    theta = angles(np.abs(freqs), np.arange(SAMPLES), SAMPLES)
    sign = np.where(freqs < 0, -1.0, 1.0)[:, None]
    back_y = np.concatenate(
        [
            np.concatenate([np.cos(theta), sign * np.sin(theta)], axis=1),
            np.concatenate([-np.sin(theta), sign * np.cos(theta)], axis=1),
        ],
        axis=0,
    )
    shift = np.arange(N)
    bell = np.ones(N)
    for freq in range(1, 256):
        bell += 2.0 * np.cos(2.0 * np.pi / N * ((freq * shift) % N))
    bell /= SAMPLES
    bell += np.cos(2.0 * np.pi / N * ((256 * shift) % N)) / SAMPLES
    spread = bell[(pixels[None, :] - 8 * np.arange(SAMPLES)[:, None]) % N]
    pick = np.zeros((512, 256))
    for row in range(KEEP):
        a = abs(row - HALF)
        if a < HALF:
            pick[row, 16 * (a // 8) + a % 8] = 1.0
            pick[KEEP + row, 16 * (a // 8) + 8 + a % 8] = 1.0
    flip = np.zeros((KEEP, KEEP))
    for lane in range(1, KEEP):
        flip[KEEP - lane, lane] = 1.0
    return {
        "ahead": ahead.astype(bfloat16),
        "ahead_x": ahead_x.astype(bfloat16),
        "back_x": back_x.astype(bfloat16),
        "back_y": back_y.astype(bfloat16),
        "spread": spread.astype(bfloat16),
        "spread_t": np.ascontiguousarray(spread.T).astype(bfloat16),
        "pick": pick.astype(bfloat16),
        "merge": np.ascontiguousarray(pick.T).astype(bfloat16),
        "flip": flip.astype(bfloat16),
    }


def dot_nn(left, right):
    return lax.dot_general(left, right, (((1,), (0,)), ((), ())), preferred_element_type=F32)


def dot_nt(left, right):
    return lax.dot_general(left, right, (((1,), (1,)), ((), ())), preferred_element_type=F32)


def iota(shape, axis):
    return lax.broadcasted_iota(jnp.int32, shape, axis)


def each(low, high, body):
    for i in range(low, high):
        body(i)


def rem(value, by):
    return value % by if isinstance(value, int) else lax.rem(value, by)


def div(value, by):
    return value // by if isinstance(value, int) else lax.div(value, by)


def place():
    tile = lax.axis_index("tile")
    mask = lax.axis_index("mask")
    pencil = lax.axis_index("pencil")
    return tile, mask, pencil, div(pencil, 8), rem(pencil, 8)


def remote(src, dst, send, recv, where):
    return pltpu.make_async_remote_copy(
        src_ref=src, dst_ref=dst, send_sem=send, recv_sem=recv, device_id=where, device_id_type=MESH
    )


def step_kernel(
    mask_hbm, ahead_hbm, ahead_x_hbm, back_x_hbm, back_y_hbm, spread_hbm, target_hbm, spread_t_hbm,
    pick_ref, merge_ref, flip_ref, spectra_ref, points_ref, weights_ref, radii_ref,
    gradient_hbm, scale_out, loss_out,
    mask_ref, ahead_ref, ahead_x_ref, back_x, back_y, spread, target, spread_t,
    line_ref, lines_ref, seen, kern, slices, bands, fields, gap_ref, slope_ref, hot_ref, hot_t_ref,
    part_ref, gathered, summed, pieces, whole, note, notes, rounds, totals,
    load_sem, self_sem, kz_send, kz_recv, ka_send, ka_recv, kb_send, kb_recv, kd_send, kd_recv, ke_send, ke_recv, kc_send, kc_recv,
    a_send, a_recv, sz_send, sz_recv, sy_send, sy_recv,
    cy_send, cy_recv, cz_send, cz_recv, dz_send, dz_recv, dy_send, dy_recv, e_send, e_recv, f_send, f_recv, g_send, g_recv,
):
    tile, mask, pencil, y, z = place()
    chip, core = (div(tile, 2), rem(tile, 2))
    owner = (z >= FIRST) & (z < FIRST + 4)
    column = z - FIRST
    load_mask = pltpu.make_async_copy(mask_hbm, mask_ref, load_sem.at[0])
    load_ahead = pltpu.make_async_copy(ahead_hbm, ahead_ref, load_sem.at[1])
    load_mask.start()
    load_ahead.start()
    barrier = pltpu.get_barrier_semaphore()

    def greet(where):
        pl.semaphore_signal(barrier, inc=1, device_id=where, device_id_type=MESH)

    each(1, 32, lambda d: greet({"pencil": rem(pencil + d, 32)}))
    each(0, 8, lambda d: greet({"mask": 1 - mask, "pencil": y * 8 + d}))
    each(1, 8, lambda d: greet({"tile": rem(tile + d, 8)}))

    sub = iota((8, KEEP), 0)
    lane = iota((8, KEEP), 1)
    freq_u = lane - HALF
    freq_v = sub + pencil * 8 - HALF
    radius = freq_u * freq_u + freq_v * freq_v
    parts = []
    for c in range(2):
        for k in range(KERN):
            limit = radii_ref[k] * radii_ref[k]
            parts.append(jnp.where(radius <= limit, spectra_ref[c, k], 0.0))
    plain = jnp.concatenate(parts, axis=0)
    turned = dot_nn(plain.astype(BF16), flip_ref[...])
    sign = jnp.where(iota((64, KEEP), 0) < 32, 1.0, -1.0)
    low = jnp.where(pencil < 16, 1.0, 0.0).astype(F32)
    plain = low * (turned * sign) + (1.0 - low) * plain
    spare = (sub == 1) & (lane == 0) & (pencil == 16)
    for part in range(8):
        rows = plain[part * 8 : part * 8 + 8]
        rest = rows - rows.astype(BF16).astype(F32)
        rows = jnp.where(spare, rest[0:1, HALF : HALF + 1], rows)
        slices[part] = jnp.concatenate([rows[:, :HALF], rows[:, HALF:]], axis=0).astype(BF16)
    kern[core, chip, y, z] = slices[tile]

    point_rows = points_ref[0].astype(F32) - (pencil * ROWS).astype(F32)
    point_cols = points_ref[1].astype(F32)
    normal = points_ref[2]
    step_row = jnp.where(normal == 0, 1.0, 0.0) - jnp.where(normal == 1, 1.0, 0.0)
    step_col = jnp.where(normal == 2, 1.0, 0.0) - jnp.where(normal == 3, 1.0, 0.0)
    flat = jnp.concatenate(
        [
            point_rows, point_rows - step_row, point_rows + step_row,
            point_cols, point_cols - step_col, point_cols + step_col,
            weights_ref[...], jnp.zeros((1, PTS), F32),
        ],
        axis=0,
    )
    tall = flat.T
    cols = jnp.concatenate([tall[:, 3:4], tall[:, 4:5], tall[:, 5:6]], axis=0).astype(jnp.int32)
    wide_rows = jnp.concatenate([flat[0:1], flat[1:2], flat[2:3]], axis=1).astype(jnp.int32)
    wide_cols = jnp.concatenate([flat[3:4], flat[4:5], flat[5:6]], axis=1).astype(jnp.int32)
    weight = jnp.concatenate([weights_ref[...]] * 3, axis=1)
    third = iota((1, 3 * PTS), 1)
    goal = jnp.where(third < PTS, 0.5, jnp.where(third < 2 * PTS, 1.0, 0.0))
    row_hot = jnp.where(iota((ROWS, 3 * PTS), 0) == wide_rows, 1.0, 0.0)

    load_mask.wait()
    load_ahead.wait()
    later = [
        pltpu.make_async_copy(ahead_x_hbm, ahead_x_ref, load_sem.at[2]),
        pltpu.make_async_copy(back_x_hbm.at[pencil], back_x, load_sem.at[3]),
        pltpu.make_async_copy(back_y_hbm, back_y, load_sem.at[4]),
        pltpu.make_async_copy(spread_hbm, spread, load_sem.at[5]),
        pltpu.make_async_copy(target_hbm, target, load_sem.at[6]),
        pltpu.make_async_copy(spread_t_hbm, spread_t, load_sem.at[7]),
    ]
    for load in later:
        load.start()
    line = dot_nt(ahead_ref[...], mask_ref[...].astype(BF16))
    lane8 = iota((8, ROWS), 1)
    cosine, sine = (line[256:264], line[264:272])
    both = jnp.where(lane8 < 64, cosine + pltpu.roll(cosine, 64, 1), sine + pltpu.roll(sine, 64, 1))
    empty = jnp.where(iota((8, ROWS), 0) == 0, both, line[8:16])
    line_ref[...] = jnp.concatenate([line[:8], empty, line[16:256]], axis=0).astype(BF16)

    pl.semaphore_wait(barrier, 46)

    def hop(rows, send, recv, other, spot, where):
        return remote(rows, rows, send.at[other], recv.at[spot], where)

    def kz(d, theirs=False):
        other = rem(z + d, 8)
        spot = other if theirs else z
        return hop(kern.at[core, chip, y, spot], kz_send, kz_recv, other, spot, {"pencil": y * 8 + other})

    def along_x(d, theirs):
        other = rem(chip + d, 4)
        return other, other if theirs else chip, {"tile": other * 2 + core}

    def along_y(d, theirs):
        other = rem(y + d, 4)
        return other, other if theirs else y, {"pencil": other * 8 + z}

    def ka(d, theirs=False):
        other, spot, where = along_x(d, theirs)
        return hop(kern.at[core, spot, y, pl.ds(0, 4)], ka_send, ka_recv, other, spot, where)

    def kb(d, theirs=False):
        other, spot, where = along_y(d, theirs)
        return hop(kern.at[core, chip, spot, pl.ds(4, 4)], kb_send, kb_recv, other, spot, where)

    def kd(d, theirs=False):
        other, spot, where = along_y(d, theirs)
        return hop(kern.at[core, pl.ds(0, 4), spot, pl.ds(0, 4)], kd_send, kd_recv, other, spot, where)

    def ke(d, theirs=False):
        other, spot, where = along_x(d, theirs)
        return hop(kern.at[core, spot, pl.ds(0, 4), pl.ds(4, 4)], ke_send, ke_recv, other, spot, where)

    def kc(half, theirs=False):
        side = 1 - core if theirs else core
        rows = kern.at[side, pl.ds(0, 4), pl.ds(0, 4), pl.ds(4 * half, 4)]
        return remote(rows, rows, kc_send.at[half], kc_recv.at[half], {"tile": chip * 2 + 1 - core})

    each(1, 8, lambda d: kz(d).start())

    own_lines = lines_ref.at[:, pl.ds(pl.multiple_of(pencil * ROWS, ROWS), ROWS)]

    def line_to(d):
        q = rem(div(pencil, 2) + d, 16)
        home = div(q, 4) * 8 + FIRST + rem(q, 4)
        src = line_ref.at[pl.ds(pl.multiple_of(q * 16, 16), 16)]
        return home, remote(src, own_lines, a_send.at[q], a_recv, {"pencil": home})

    def send_line(d):
        home, copy = line_to(d)

        @pl.when(home != pencil)
        def _():
            copy.start()

    each(0, 16, send_line)

    @pl.when(owner)
    def _():
        src = line_ref.at[pl.ds(pl.multiple_of((y * 4 + column) * 16, 16), 16)]
        keep = pltpu.make_async_copy(src, own_lines, self_sem)
        keep.start()
        keep.wait()

    each(1, 8, lambda d: kz(d, True).wait_recv())
    each(1, 4, lambda d: ka(d).start())
    each(1, 4, lambda d: kb(d).start())

    down = wide_cols - iota((128, 3 * PTS), 0)
    for base in range(0, N, 128):
        hot_t_ref[base : base + 128, :] = jnp.where(down == base, 1.0, 0.0).astype(BF16)

    each(1, 4, lambda d: ka(d, True).wait_recv())
    each(1, 4, lambda d: kd(d).start())
    each(1, 4, lambda d: kb(d, True).wait_recv())
    each(1, 4, lambda d: ke(d).start())

    def sz(d):
        side = mask if d < 8 else 1 - mask
        other = rem(z + d, 8)
        mine = seen.at[y, mask, column]
        where = {"mask": side, "pencil": y * 8 + other}
        return remote(mine, mine, sz_send.at[side * 8 + other], sz_recv.at[mask * 4 + column], where)

    later[0].wait()

    @pl.when(owner)
    def _():
        others = lines_ref.at[:, pl.ds(0, 31 * ROWS)]
        remote(others, others, a_send.at[0], a_recv, {"pencil": rem(pencil + 1, 32)}).wait_recv()
        held = lines_ref[...].astype(F32)
        first = (y == 0) & (column == 0)
        stash = (iota((16, N), 0) == 8) & first
        extra = jnp.where(stash, held, 0.0)
        left = (iota((16, N), 1) % 128) < 64
        cos_sum = jnp.sum(jnp.where(left, extra, 0.0))
        sin_sum = jnp.sum(jnp.where(left, 0.0, extra))
        out = dot_nn(jnp.where(stash, 0.0, held).astype(BF16), ahead_x_ref[...])
        real = out[:8, :KEEP] + out[8:, KEEP:]
        imag = out[8:, :KEEP] - out[:8, KEEP:]
        slot = (sub == 0) & (lane == HALF + 1) & first
        real = jnp.where(slot, cos_sum, real)
        imag = jnp.where(slot, sin_sum, imag)
        still = (sub == 0) & (lane == HALF) & first
        imag = jnp.where(still, real - real.astype(BF16).astype(F32), imag)
        piece = jnp.concatenate([real, imag], axis=0) * (1.0 / (N * N))
        seen[y, mask, column] = piece.astype(BF16)
        each(1, 16, lambda d: sz(d).start())

    across = jnp.broadcast_to(cols, (3 * PTS, 128)) - iota((3 * PTS, 128), 1)
    for base in range(0, N, 128):
        hot_ref[:, base : base + 128] = jnp.where(across == base, 1.0, 0.0).astype(BF16)

    each(1, 4, lambda d: kd(d, True).wait_recv())
    kc(0).start()
    each(1, 4, lambda d: ke(d, True).wait_recv())
    kc(1).start()

    def sz_wait(m, q):
        theirs = seen.at[y, m, q]
        mine = (m == mask) & (q == column)

        @pl.when(jnp.logical_not(mine))
        def _():
            where = {"pencil": y * 8 + rem(z + 1, 8)}
            remote(theirs, theirs, sz_send.at[q], sz_recv.at[m * 4 + q], where).wait_recv()

    def sy(d, m, theirs=False):
        other = rem(y + d, 4)
        spot = other if theirs else y
        rows = seen.at[spot, m]
        return remote(rows, rows, sy_send.at[m, other], sy_recv.at[m, spot], {"pencil": other * 8 + z})

    def forward(m):
        each(0, 4, lambda q: sz_wait(m, q))
        each(1, 4, lambda d: sy(d, m).start())

    forward(mask)
    forward(1 - mask)
    kc(0, True).wait_recv()
    kc(1, True).wait_recv()

    slot = (sub == 0) & (lane == HALF + 1)
    still = (sub == 0) & (lane == HALF)

    for part in range(8):
        lines = kern[part % 2, part // 2].astype(F32).reshape(PENCIL, 16, HALF)
        bands[part] = jnp.concatenate(
            [lines[:, :8].reshape(KEEP, HALF), lines[:, 8:].reshape(KEEP, HALF)], axis=1
        )
        middle = bands[part, HALF : HALF + 8]
        rest = middle[1:2, 0:1]
        middle = jnp.where(still, middle + rest, jnp.where((sub == 1) & (lane == 0), 0.0, middle))
        bands[part, HALF : HALF + 8] = middle

    def spectrum(which):
        held = jnp.concatenate([seen[i, which].reshape(64, KEEP) for i in range(4)], axis=0)
        full = dot_nn(pick_ref[...], held)
        real, imag = (full[:KEEP], full[KEEP:])
        mid_real, mid_imag = (real[HALF : HALF + 8], imag[HALF : HALF + 8])
        edge_real = jnp.sum(jnp.where(slot, mid_real, 0.0))
        edge_imag = jnp.sum(jnp.where(slot, mid_imag, 0.0))
        mid_real = jnp.where(slot, pltpu.roll(mid_real, 2, 1), mid_real)
        mid_imag = jnp.where(slot, -pltpu.roll(mid_imag, 2, 1), mid_imag)
        mid_real = jnp.where(still, mid_real + mid_imag, mid_real)
        mid_imag = jnp.where(still, 0.0, mid_imag)
        top_real = jnp.where(sub == 0, edge_real, real[:8])
        top_imag = jnp.where(sub == 0, edge_imag, imag[:8])
        real = jnp.concatenate([top_real, real[8:HALF], mid_real, real[HALF + 8 :]], axis=0)
        imag = jnp.concatenate([top_imag, imag[8:HALF], mid_imag, imag[HALF + 8 :]], axis=0)
        return real, imag

    def remainder(band):
        middle = band[HALF : HALF + 8]
        return (middle - middle.astype(BF16).astype(F32))[0:1, HALF : HALF + 1]

    for load in later[1:]:
        load.wait()
    images = []
    for turn in range(2):
        which = mask if turn == 0 else 1 - mask
        each(1, 4, lambda d, which=which: sy(d, which, True).wait_recv())
        real, imag = spectrum(which)
        columned, rests, rests_imag = ([], [], [])
        for k in range(KERN):
            kern_real, kern_imag = (bands[k], bands[KERN + k])
            band_real = kern_real * real - kern_imag * imag
            band_imag = kern_real * imag + kern_imag * real
            band = jnp.concatenate([band_real, band_imag], axis=1).astype(BF16)
            out = dot_nt(back_x[...], band)
            out = jnp.concatenate([out[:ROWS], out[ROWS:]], axis=1)
            rounded = out.astype(BF16)
            columned.append(rounded)
            rest = out - rounded.astype(F32)
            rests.append(rest[:, HALF : HALF + 1] + remainder(band_real))
            rests_imag.append(rest[:, KEEP + HALF : KEEP + HALF + 1] + remainder(band_imag))
        field = dot_nn(jnp.concatenate(columned, axis=0), back_y[...])
        rest_real = jnp.broadcast_to(jnp.concatenate(rests, axis=0), (512, SAMPLES))
        rest_imag = jnp.broadcast_to(jnp.concatenate(rests_imag, axis=0), (512, SAMPLES))
        field = field + jnp.concatenate([rest_real, rest_imag], axis=1)
        if turn == 0:
            fields[...] = field.astype(BF16)
        square = field * field
        square = square[:, :SAMPLES] + square[:, SAMPLES:]
        images.append(square[:128] + square[128:256] + square[256:384] + square[384:])
    image = jnp.concatenate(images, axis=0).astype(BF16)

    loss = jnp.zeros((ROWS, 128), F32)
    picked = jnp.zeros((ROWS, 3 * PTS), F32)
    for base in range(0, N, CHUNK):
        at = slice(base, base + CHUNK)
        fine = dot_nn(image, spread[:, at])
        clear = 0.5 - 0.5 * jnp.tanh(3.0 * fine - 1.5)
        own, other = (clear[:ROWS], clear[ROWS:])
        product = own * other
        union = 1.0 - product
        slope_ref[:, at] = 12.0 * product * (1.0 - own)
        gap = union - target[:, at].astype(F32)
        gap_ref[:, at] = gap
        picked = picked + dot_nn(union.astype(BF16), hot_t_ref[at, :])
        square = gap * gap
        loss = loss + (square[:, :128] + square[:, 128:256]) + (square[:, 256:384] + square[:, 384:])
    missed = jnp.sum(picked * row_hot, axis=0, keepdims=True) - goal
    push = weight * missed
    loss = jnp.sum(loss) + jnp.sum(push * missed)
    hits = (row_hot * push).astype(BF16)
    drive = jnp.zeros((ROWS, SAMPLES), F32)
    for base in range(0, N, CHUNK):
        at = slice(base, base + CHUNK)
        pull = gap_ref[:, at] + dot_nn(hits, hot_ref[:, at])
        drive = drive + dot_nn((pull * slope_ref[:, at]).astype(BF16), spread_t[at, :])
    sum_real = jnp.zeros((KEEP, KEEP), F32)
    sum_imag = jnp.zeros((KEEP, KEEP), F32)
    wide_drive = jnp.concatenate([drive, drive], axis=1)
    for pair in range(0, KERN, 2):
        mixed = [
            (wide_drive * fields[k * ROWS : k * ROWS + ROWS].astype(F32)).astype(BF16) for k in (pair, pair + 1)
        ]
        lines = dot_nt(back_y[...], jnp.concatenate(mixed, axis=0))
        for k in (pair, pair + 1):
            at = slice((k - pair) * ROWS, (k - pair + 1) * ROWS)
            line = jnp.concatenate([lines[:KEEP, at], lines[KEEP:, at]], axis=1).astype(BF16)
            back = dot_nn(line, back_x[...])
            back_real, back_imag = (back[:, :KEEP], back[:, KEEP:])
            kern_real, kern_imag = (bands[k], bands[KERN + k])
            sum_real = sum_real + (kern_real * back_real + kern_imag * back_imag)
            sum_imag = sum_imag + (kern_real * back_imag - kern_imag * back_real)
    sum_real = sum_real * (2.0 / (N * N))
    sum_imag = sum_imag * (2.0 / (N * N))

    mid_real, mid_imag = (sum_real[HALF : HALF + 8], sum_imag[HALF : HALF + 8])
    turned = dot_nn(jnp.concatenate([mid_real, mid_imag], axis=0).astype(BF16), flip_ref[...])
    edge_real = jnp.sum(jnp.where(still, sum_real[:8], 0.0))
    edge_imag = jnp.sum(jnp.where(still, sum_imag[:8], 0.0))
    fold_real = jnp.where(lane < HALF, mid_real + turned[:8], jnp.where(lane == HALF, mid_real, 0.0))
    fold_imag = jnp.where(lane < HALF, mid_imag - turned[8:], 0.0)
    fold_real = jnp.where(lane == HALF + 1, edge_real, jnp.where(lane == HALF + 2, loss, fold_real))
    fold_imag = jnp.where(lane == HALF + 1, edge_imag, fold_imag)
    mid_real = jnp.where(sub == 0, fold_real, mid_real)
    mid_imag = jnp.where(sub == 0, fold_imag, mid_imag)
    full = jnp.concatenate(
        [
            sum_real[:HALF], mid_real, sum_real[HALF + 8 :],
            sum_imag[:HALF], mid_imag, sum_imag[HALF + 8 :],
        ],
        axis=0,
    ).astype(BF16)
    part_ref[...] = dot_nn(merge_ref[...], full).astype(BF16).reshape(4, 4, 16, KEEP)

    def cy(d, theirs=False):
        other = rem(y + d, 4)
        spot = other if theirs else y
        where = {"pencil": other * 8 + z}
        return remote(part_ref.at[other], gathered.at[spot], cy_send.at[other], cy_recv.at[spot], where)

    each(1, 4, lambda d: cy(d).start())
    gathered[y] = part_ref[y]
    each(1, 4, lambda d: cy(d, True).wait_recv())
    total = gathered[0].astype(F32) + gathered[1].astype(F32)
    total = total + (gathered[2].astype(F32) + gathered[3].astype(F32))
    summed[...] = total.astype(BF16)

    def cz(q):
        home = FIRST + q
        return home, remote(summed.at[q], pieces.at[z], cz_send.at[q], cz_recv.at[z], {"pencil": y * 8 + home})

    def send_piece(q):
        home, copy = cz(q)

        @pl.when(home != z)
        def _():
            copy.start()

    each(0, 4, send_piece)

    def dz(d):
        other = rem(z + d, 8)
        mine = whole.at[y, column]
        return remote(mine, mine, dz_send.at[other], dz_recv.at[column], {"pencil": y * 8 + other})

    row = iota((16, KEEP), 0)
    lane = iota((16, KEEP), 1)
    note_row = iota((8, 128), 0)

    def tell(d, theirs=False):
        other = rem(tile + d, 8)
        spot = other if theirs else tile
        return remote(note, notes.at[spot], e_send.at[other], e_recv.at[spot], {"tile": other})

    @pl.when(owner)
    def _():
        pieces[z] = summed[column]

        def piece_from(d):
            other = rem(z + d, 8)
            where = {"pencil": y * 8 + other}
            return remote(summed.at[0], pieces.at[other], cz_send.at[0], cz_recv.at[other], where)

        each(1, 8, lambda d: piece_from(d).wait_recv())
        one = pieces[...].astype(F32)
        one = (one[0] + one[1]) + (one[2] + one[3]) + (one[4] + one[5]) + (one[6] + one[7])
        whole[y, column] = one.astype(BF16)
        first = (y == 0) & (column == 0)
        loss = jnp.sum(jnp.where(first & (row == 0) & (lane == HALF + 2), one, 0.0))
        stash = first & ((row == 0) | (row == 8)) & (lane > HALF + 1)
        center = first & (row == 0) & (lane == HALF)
        energy = jnp.where(stash, 0.0, one * one) * jnp.where(center, 1.0, 0.5)
        energy = jnp.sum(energy)
        note[...] = jnp.where(note_row == 0, energy, jnp.where(note_row == 1, loss, 0.0))
        each(1, 8, lambda d: tell(d).start())
        notes[tile] = note[...]
        each(1, 8, lambda d: dz(d).start())

    def dz_wait(q):
        theirs = whole.at[y, q]

        @pl.when(q != column)
        def _():
            where = {"pencil": y * 8 + rem(z + 1, 8)}
            remote(theirs, theirs, dz_send.at[q], dz_recv.at[q], where).wait_recv()

    def dy(d, theirs=False):
        other = rem(y + d, 4)
        spot = other if theirs else y
        rows = whole.at[spot]
        return remote(rows, rows, dy_send.at[other], dy_recv.at[spot], {"pencil": other * 8 + z})

    def share(step):
        d = 8 + div(step, 2) * (1 if step % 2 else -1)
        spot = rem(mask * 8 + z + d, 16)
        mine = rounds.at[mask * 4 + column]
        where = {"mask": div(spot, 8), "pencil": y * 8 + rem(spot, 8)}
        return remote(mine, mine, f_send.at[spot], f_recv.at[mask * 4 + column], where)

    @pl.when(owner)
    def _():
        each(1, 8, lambda d: tell(d, True).wait_recv())
        rounds[mask * 4 + column] = jnp.sum(notes[...], axis=0)
        each(1, 16, lambda d: share(d).start())

    each(0, 4, dz_wait)
    each(1, 4, lambda d: dy(d).start())

    def share_wait(s):
        theirs = rounds.at[s]

        @pl.when(jnp.logical_not((s // 4 == mask) & (s % 4 == column)))
        def _():
            where = {"pencil": y * 8 + rem(z + 1, 8)}
            remote(theirs, theirs, f_send.at[s], f_recv.at[s], where).wait_recv()

    each(0, 8, share_wait)
    totals[y] = jnp.sum(rounds[...], axis=0)

    def fy(d, theirs=False):
        other = rem(y + d, 4)
        spot = other if theirs else y
        rows = totals.at[spot]
        return remote(rows, rows, g_send.at[other], g_recv.at[spot], {"pencil": other * 8 + z})

    each(1, 4, lambda d: fy(d).start())

    each(1, 4, lambda d: dy(d, True).wait_recv())

    band = whole[...].astype(F32).reshape(KEEP, KEEP)
    head = band[:16]
    edge_real = jnp.sum(jnp.where((row == 0) & (lane == HALF + 1), head, 0.0))
    edge_imag = jnp.sum(jnp.where((row == 8) & (lane == HALF + 1), head, 0.0))
    head = jnp.where(((row == 0) | (row == 8)) & (lane > HALF), 0.0, head)
    band = jnp.concatenate([head, band[16:]], axis=0)
    pairs = band.reshape(16, 2, 8, KEEP)
    turned = jnp.concatenate([pairs[:, 1:2], -pairs[:, 0:1]], axis=1).reshape(KEEP, KEEP)
    stacked = jnp.concatenate([band, turned], axis=1).astype(BF16)
    lines = dot_nt(back_x[0:ROWS], stacked).astype(BF16)
    for base in range(0, N, CHUNK):
        at = slice(base, base + CHUNK)
        extra = ahead_ref[256:272, at].astype(F32)
        extra = edge_real * extra[0:1] + edge_imag * extra[8:9]
        target[:, at] = (dot_nn(lines, ahead_ref[0:256, at]) + extra).astype(BF16)
    store = pltpu.make_async_copy(target, gradient_hbm, load_sem.at[0])
    store.start()

    each(1, 8, lambda d: kz(d).wait_send())
    for step in (ka, kb, kd, ke):
        each(1, 4, lambda d, step=step: step(d).wait_send())
    kc(0).wait_send()
    kc(1).wait_send()
    each(1, 4, lambda d: sy(d, 0).wait_send())
    each(1, 4, lambda d: sy(d, 1).wait_send())
    each(1, 4, lambda d: cy(d).wait_send())
    each(1, 4, lambda d: dy(d).wait_send())

    def sent_line(d):
        home, copy = line_to(d)

        @pl.when(home != pencil)
        def _():
            copy.wait_send()

    each(0, 16, sent_line)

    def sent_piece(q):
        home, copy = cz(q)

        @pl.when(home != z)
        def _():
            copy.wait_send()

    each(0, 4, sent_piece)

    @pl.when(owner)
    def _():
        each(1, 16, lambda d: sz(d).wait_send())
        each(1, 8, lambda d: dz(d).wait_send())

    each(1, 4, lambda d: fy(d, True).wait_recv())
    total = (totals[0] + totals[1]) + (totals[2] + totals[3])
    scale_out[...] = STEP_SIZE * lax.rsqrt(total[0:1] * (1.0 / 16.0) + EPSILON)
    loss_out[0, 0] = jnp.sum(jnp.where(note_row == 1, total, 0.0)) * (0.5 / (128.0 * 8.0 * N * N))
    store.wait()
    each(1, 4, lambda d: fy(d).wait_send())

    @pl.when(owner)
    def _():
        each(1, 8, lambda d: tell(d).wait_send())
        each(1, 16, lambda d: share(d).wait_send())


ANY_SPEC = pl.BlockSpec(memory_space=pl.ANY)
VMEM_SPEC = pl.BlockSpec(memory_space=VMEM)
SMEM_SPEC = pl.BlockSpec(memory_space=pltpu.SMEM)
LIMIT = 56 * 1024 * 1024


def per_device(mask_field, design_target, kernel_spectra, support_radii, edge_points, point_weights):
    table = {name: jnp.asarray(value) for name, value in tables().items()}
    plane = mask_field.reshape(ROWS, N)
    gradient, scale, loss = pl.pallas_call(
        step_kernel,
        out_shape=(
            jax.ShapeDtypeStruct((ROWS, N), BF16),
            jax.ShapeDtypeStruct((1, 128), F32),
            jax.ShapeDtypeStruct((1, 1), F32),
        ),
        in_specs=[ANY_SPEC] * 8 + [VMEM_SPEC] * 6 + [SMEM_SPEC],
        out_specs=(ANY_SPEC, VMEM_SPEC, SMEM_SPEC),
        scratch_shapes=[
            VMEM((ROWS, N), F32),
            VMEM((272, N), BF16),
            VMEM((N, 512), BF16),
            VMEM((256, 512), BF16),
            VMEM((512, 1024), BF16),
            VMEM((SAMPLES, N), BF16),
            VMEM((ROWS, N), BF16),
            VMEM((N, SAMPLES), BF16),
            VMEM((256, ROWS), BF16),
            VMEM((16, N), BF16),
            VMEM((4, 2, 4, 16, KEEP), BF16),
            VMEM((2, 4, 4, 8, 16, HALF), BF16),
            VMEM((8, 16, HALF), BF16),
            VMEM((8, KEEP, KEEP), F32),
            VMEM((512, 1024), BF16),
            VMEM((ROWS, N), F32),
            VMEM((ROWS, N), F32),
            VMEM((3 * PTS, N), BF16),
            VMEM((N, 3 * PTS), BF16),
            VMEM((4, 4, 16, KEEP), BF16),
            VMEM((4, 4, 16, KEEP), BF16),
            VMEM((4, 16, KEEP), BF16),
            VMEM((8, 16, KEEP), BF16),
            VMEM((4, 4, 16, KEEP), BF16),
            VMEM((8, 128), F32),
            VMEM((8, 8, 128), F32),
            VMEM((8, 8, 128), F32),
            VMEM((4, 8, 128), F32),
            DMA((8,)),
            DMA,
        ]
        + [DMA((8,))] * 2
        + [DMA((4,))] * 8
        + [DMA((2,))] * 2
        + [DMA((16,)), DMA, DMA((16,)), DMA((8,)), DMA((2, 4)), DMA((2, 4))]
        + [DMA((4,)), DMA((4,)), DMA((4,)), DMA((8,)), DMA((8,)), DMA((4,)), DMA((4,)), DMA((4,))]
        + [DMA((8,)), DMA((8,)), DMA((16,)), DMA((8,)), DMA((4,)), DMA((4,))],
        compiler_params=pltpu.CompilerParams(collective_id=0, has_side_effects=True, vmem_limit_bytes=LIMIT),
        name="step_kernel",
    )(
        plane, table["ahead"], table["ahead_x"], table["back_x"], table["back_y"], table["spread"],
        design_target.reshape(ROWS, N), table["spread_t"], table["pick"], table["merge"], table["flip"],
        kernel_spectra, edge_points.reshape(3, 1, PTS), point_weights, support_radii,
    )
    update = (plane - scale[0, 0] * gradient.astype(F32)).astype(BF16)
    return update.reshape(1, 1, ROWS, N), loss.reshape(())


def solution(mesh):
    placed = (
        P("tile", "mask", "pencil", None),
        P("tile", "pencil", None),
        P(None, None, "pencil", None),
        P(),
        P("tile", None, "pencil"),
        P("tile", "pencil"),
    )
    return jax.shard_map(
        per_device,
        mesh=mesh,
        in_specs=placed,
        out_specs=(P("tile", "mask", "pencil", None), P()),
        check_vma=False,
    )
```
